32 devices in a mesh: lat: 16 (over z, y, core), lon: 2 (over x).
Axes of the slice: x: 2, y: 2, z: 4, core: 2. Of those that a mesh axis runs over, the one named last changes fastest.
Arguments:
- field: bfloat16 [192, 768, 512], P('lat', 'lon'), may hold values from -6 to 6
- quad_weight: float32 [192], P('lat'), may hold values from 0.5 to 1.5
- legendre: bfloat16 [192, 192, 192], P('lat'), as said below
- filter_real: float32 [192, 512], replicated, may hold values from -4 to 4
- filter_imag: float32 [192, 512], replicated, may hold values from -4 to 4
- neighbour: int32 [192, 12], P('lat'), may hold values from 0 to 24
- basis: int32 [192, 12], P('lat'), may hold values from 0 to 7
- disco_quad: float32 [192, 12], P('lat'), may hold values from 0.5 to 1.5
- disco_weight: float32 [8, 512], replicated, may hold values from -2 to 2
- norm_gain: float32 [512], replicated, may hold values from 0.5 to 1.5
- w_in: bfloat16 [512, 1024], replicated, may hold values from -0.25 to 0.25
- b_in: float32 [1024], replicated, may hold values from -3 to 3
- w_out: bfloat16 [1024, 512], replicated, may hold values from -0.1875 to 0.1875
- b_out: float32 [512], replicated, may hold values from -3 to 3
Outputs:
- block_out: bfloat16 [192, 768, 512], P('lat', 'lon')
- spatial: bfloat16 [192, 768, 512], P('lat', 'lon')
The draws below stay inside these ranges and needn't reach their ends.
Inputs may be any that keep to these rules, and one draw needn't show every extreme that they name: legendre[m, l, t] = 0 for l < m.
All inputs are finite; a program needn't handle non-finite values.
Results may differ from the reference program's by a relative error of at most 0.018.
Values may be sent and summed in bfloat16 or wider, within the bound.
No kernel may reach another device: no remote copies, remote signals or barrier semaphores. Data moves between devices by JAX's collectives and lax.ppermute only.
A program may use at most 64 MiB of HBM per device.

```python
import math
import jax
import jax.numpy as jnp
from jax import lax

C = 512
FF = 1024
NLON = 768
HALO = 2
SLOTS = 12
KB = 8
NLAT = 192
MMAX = 192
LMAX = 192
NWIN = 25


def draw_legendre(key, part):
    values = jax.random.normal(key, (MMAX, LMAX, NLAT), jnp.float32)
    values = values * NLAT ** (-0.5)
    waves = jnp.arange(MMAX, dtype=jnp.int32)[:, None, None]
    degrees = jnp.arange(LMAX, dtype=jnp.int32)[None, :, None]
    values = jnp.where(degrees >= waves, values, 0.0)
    return values.astype(jnp.bfloat16)


def set_ends(drawn, key, smallest, largest):
    extent = drawn.shape
    place = [jax.random.randint(jax.random.fold_in(key, axis), (), 0, extent[axis]) for axis in range(len(extent))]
    drawn = drawn.at[tuple(place)].set(smallest)
    longest = extent.index(max(extent))
    place[longest] = (place[longest] + 1) % extent[longest]
    return drawn.at[tuple(place)].set(largest)


def levels(stream_key, extent, cuts, low, top_value):
    loudness = 1.0
    for dim, parts in cuts:
        draws = jax.random.uniform(jax.random.fold_in(jax.random.fold_in(stream_key, 6), dim), (parts,), jnp.float32, low / len(cuts), top_value / len(cuts))
        loudness = loudness * jnp.repeat(jnp.exp(draws), extent[dim] // parts).reshape((-1,) + (1,) * (len(extent) - 1 - dim))
    return loudness


def bell_draw(key, extent, width, limit, cuts=(), kind=jnp.bfloat16):
    gain = levels(key, extent, cuts, -0.22, 0.18) if cuts else 1.0
    entries = jax.random.normal(key, extent, jnp.float32) * width * gain
    return jnp.minimum(jnp.maximum(entries, -limit), limit).astype(kind)


def setup_inputs(seed: int = 0) -> dict:
    splits = jax.random.split(jax.random.key(seed), 15)
    return {
        "field": bell_draw(splits[0], (NLAT, NLON, C), 1.0, 6.0, ((0, 16), (1, 2))),
        "quad_weight": jnp.clip(0.5 + 1.0 * jax.random.uniform(splits[1], (NLAT,), jnp.float32) ** levels(splits[1], (NLAT,), ((0, 16),), -0.2, 0.2), 0.5, 1.5),
        "legendre": draw_legendre(jax.random.fold_in(splits[14], 71), 0),
        "filter_real": bell_draw(splits[3], (LMAX, C), 0.7, 4.0, (), jnp.float32),
        "filter_imag": bell_draw(splits[4], (LMAX, C), 0.7, 4.0, (), jnp.float32),
        "neighbour": set_ends(jax.random.randint(splits[5], (NLAT, SLOTS), 0, NWIN), jax.random.fold_in(splits[5], 1), 0, NWIN - 1).astype(jnp.int32),
        "basis": set_ends(jax.random.randint(splits[6], (NLAT, SLOTS), 0, KB), jax.random.fold_in(splits[6], 1), 0, KB - 1).astype(jnp.int32),
        "disco_quad": jnp.clip(0.5 + 1.0 * jax.random.uniform(splits[7], (NLAT, SLOTS), jnp.float32) ** levels(splits[7], (NLAT, SLOTS), ((0, 16),), -0.2, 0.2), 0.5, 1.5),
        "disco_weight": bell_draw(splits[8], (KB, C), 0.3, 2.0, (), jnp.float32),
        "norm_gain": jnp.clip(1.0 + 0.1 * jax.random.normal(splits[9], (C,), jnp.float32), 0.5, 1.5),
        "w_in": bell_draw(splits[10], (C, FF), C ** -0.5, 0.25),
        "b_in": bell_draw(splits[11], (FF,), 0.5, 3.0, (), jnp.float32),
        "w_out": bell_draw(splits[12], (FF, C), FF ** -0.5, 0.1875),
        "b_out": bell_draw(splits[13], (C,), 0.5, 3.0, (), jnp.float32),
    }


exact_mode = lax.Precision.HIGHEST

def window_kernel(neighbour, basis, disco_quad, disco_weight):
    places = (neighbour[:, :, None] == jnp.arange(NWIN, dtype=jnp.int32)[None, None, :]).astype(jnp.float32)
    places = places * disco_quad[:, :, None]
    kinds = (basis[:, :, None] == jnp.arange(KB, dtype=jnp.int32)[None, None, :]).astype(jnp.float32)
    mixing = jnp.einsum('isn,isb->inb', places, kinds, precision=exact_mode)
    return jnp.einsum('inb,bc->inc', mixing, disco_weight, precision=exact_mode)

def convolve(padded, kernel, lat_rows, lon_cols):
    span = 2 * HALO + 1
    total = jnp.zeros((lat_rows, lon_cols, kernel.shape[2]), jnp.float32)
    for offset in range(NWIN):
        row_shift = offset // span
        col_shift = offset % span
        window = padded[row_shift:row_shift + lat_rows, col_shift:col_shift + lon_cols, :]
        total = total + kernel[:, offset, None, :] * window.astype(jnp.float32)
    return total

def channel_mlp(spatial, field, norm_gain, w_in, b_in, w_out, b_out):
    channels = spatial.shape[-1]
    tokens = spatial.reshape(-1, channels).astype(jnp.float32)
    center = lax.optimization_barrier(jnp.mean(tokens, axis=1, keepdims=True))
    spread = lax.optimization_barrier(jnp.mean((tokens - center) ** 2, axis=1, keepdims=True))
    normed = ((tokens - center) * lax.rsqrt(spread + 1e-05) * norm_gain).astype(jnp.bfloat16)
    hidden = jnp.dot(normed.astype(jnp.float32), w_in.astype(jnp.float32), precision=exact_mode) + b_in
    hidden = jax.nn.gelu(hidden).astype(jnp.bfloat16)
    result = jnp.dot(hidden.astype(jnp.float32), w_out.astype(jnp.float32), precision=exact_mode)
    result = result + b_out + field.reshape(-1, channels).astype(jnp.float32)
    return result.astype(jnp.bfloat16).reshape(field.shape)

def reference(field, quad_weight, legendre, filter_real, filter_imag, neighbour, basis, disco_quad, disco_weight, norm_gain, w_in, b_in, w_out, b_out):
    x_float = field.astype(jnp.float32)
    spectrum = jnp.fft.rfft(x_float, axis=1)[:, :MMAX, :] / math.sqrt(NLON)
    weight = quad_weight[:, None, None]
    weighted = jnp.stack([jnp.real(spectrum) * weight, jnp.imag(spectrum) * weight], axis=1).astype(jnp.bfloat16)
    legend = legendre.astype(jnp.float32)
    coeffs = jnp.einsum('mlt,trmc->lrmc', legend, weighted.astype(jnp.float32), precision=exact_mode)
    gain_real = filter_real[:, None, :]
    gain_imag = filter_imag[:, None, :]
    real_part = coeffs[:, 0]
    imag_part = coeffs[:, 1]
    filtered = jnp.stack([gain_real * real_part - gain_imag * imag_part, gain_real * imag_part + gain_imag * real_part], axis=1).astype(jnp.bfloat16)
    synthesis = jnp.einsum('mlt,lrmc->trmc', legend, filtered.astype(jnp.float32), precision=exact_mode).astype(jnp.bfloat16)
    modes = lax.complex(synthesis[:, 0].astype(jnp.float32), synthesis[:, 1].astype(jnp.float32))
    modes = jnp.pad(modes, ((0, 0), (0, NLON // 2 + 1 - MMAX), (0, 0)))
    wave = (jnp.fft.irfft(modes, n=NLON, axis=1) * math.sqrt(NLON)).astype(jnp.bfloat16)
    kernel = window_kernel(neighbour, basis, disco_quad, disco_weight)
    cycle = jnp.pad(wave, ((0, 0), (HALO, HALO), (0, 0)), mode='wrap')
    padded = jnp.pad(cycle, ((HALO, HALO), (0, 0), (0, 0)))
    conv = convolve(padded, kernel, NLAT, NLON)
    spatial = (wave.astype(jnp.float32) + conv).astype(jnp.bfloat16)
    block_out = channel_mlp(spatial, field, norm_gain, w_in, b_in, w_out, b_out)
    return (block_out, spatial)
```

```python
import functools
import math

import jax
import jax.numpy as jnp
import ml_dtypes
import numpy as np
from jax import lax
from jax.experimental import pallas as pl
from jax.experimental.pallas import tpu as pltpu
from jax.sharding import PartitionSpec as P

HALO = 2
SPAN = 2 * HALO + 1
NQ = 4
LANES = 128
F32 = jnp.float32
BF16 = jnp.bfloat16
VMEM_LIMIT = 56 * 1024 * 1024


def vmem_spec():
    return pl.BlockSpec(memory_space=pltpu.VMEM)


def smem_spec():
    return pl.BlockSpec(memory_space=pltpu.SMEM)


def params():
    return pltpu.CompilerParams(
        vmem_limit_bytes=VMEM_LIMIT, dimension_semantics=("arbitrary",)
    )


def cost(flops, nbytes, trans=0):
    return pl.CostEstimate(
        flops=int(flops), bytes_accessed=int(nbytes), transcendentals=int(trans)
    )


def split_np(table):
    upper = table.astype(np.float32).astype(ml_dtypes.bfloat16)
    lower = (table - upper.astype(np.float64)).astype(np.float32).astype(ml_dtypes.bfloat16)
    return upper, lower


def tables_np(nlon, lon_count, wave_block, mmax, padded_cols):
    blocks = mmax // wave_block
    waves = np.arange(mmax).reshape(blocks, 1, wave_block)
    waves = np.broadcast_to(waves, (blocks, 2, wave_block)).reshape(-1)
    imag = np.broadcast_to(np.arange(2).reshape(1, 2, 1), (blocks, 2, wave_block)).reshape(-1)

    def table(points):
        phase = (waves[:, None].astype(np.int64) * points[None, :]) % nlon
        angle = phase * (2.0 * math.pi / nlon)
        return np.where(imag[:, None] == 0, np.cos(angle), -np.sin(angle)) / math.sqrt(nlon)

    cols = nlon // lon_count
    fwd = np.stack([table(np.arange(cols) + b * cols) for b in range(lon_count)])
    factor = np.where(waves == 0, 1.0, 2.0)[:, None]
    inv = np.stack(
        [
            (factor * table((np.arange(padded_cols) - HALO + b * cols) % nlon)).T
            for b in range(lon_count)
        ]
    )
    return split_np(fwd), split_np(inv)


def dft_kernel(lon_count, cw, rows2, nz, quad_ref, *refs):
    blocks = refs[:lon_count]
    upper_ref, lower_ref, out_ref = refs[lon_count:]
    step = pl.program_id(0)
    group = rows2 if cw % LANES == 0 else 1
    wave_rows = out_ref.shape[3]
    for first in range(0, rows2, group):
        x = jnp.concatenate(
            [
                jnp.concatenate([b[first + i] for i in range(group)], axis=1)
                if group > 1
                else b[first]
                for b in blocks
            ],
            axis=0,
        )
        acc = jnp.dot(upper_ref[...], x, preferred_element_type=F32)
        acc = acc + jnp.dot(lower_ref[...], x, preferred_element_type=F32)
        for i in range(group):
            t = first + i
            scaled = acc[:, i * cw : (i + 1) * cw] * quad_ref[step * rows2 + t]
            for d in range(nz):
                for q in range(NQ):
                    at = (d * NQ + q) * wave_rows
                    out_ref[d, q, t] = scaled[at : at + wave_rows].astype(BF16)


def dft(blocks, quad, upper, lower, nz, wave_rows):
    rows, cols, cw = blocks[0].shape
    rows2 = 2
    lon_count = len(blocks)
    whole = pl.BlockSpec(upper.shape, lambda t: (0, 0))
    return pl.pallas_call(
        functools.partial(dft_kernel, lon_count, cw, rows2, nz),
        grid=(rows // rows2,),
        in_specs=[smem_spec()]
        + [pl.BlockSpec((rows2, cols, cw), lambda t: (t, 0, 0))] * lon_count
        + [whole, whole],
        out_specs=pl.BlockSpec((nz, NQ, rows2, wave_rows, cw), lambda t: (0, 0, t, 0, 0)),
        out_shape=jax.ShapeDtypeStruct((nz, NQ, rows, wave_rows, cw), BF16),
        compiler_params=params(),
        cost_estimate=cost(
            4 * upper.shape[0] * upper.shape[1] * rows * cw, 4 * rows * cols * cw * 2
        ),
    )(quad, *blocks, upper, lower)


def legendre_kernel(nz, *refs):
    own = refs[:nz]
    others = refs[nz : nz + NQ - 1]
    leg_ref, legt_ref, gr_ref, gi_ref, out_ref, wide, result = refs[nz + NQ - 1 :]
    waves, _, lat = leg_ref.shape
    rows, wave_rows, cw = out_ref.shape[2:]
    span = rows * wave_rows

    def piece(q, d):
        if q:
            return others[q - 1][d]
        return own[d][...].reshape(rows, wave_rows, cw)

    for q in range(NQ):
        for d in range(nz):
            at = (q * nz + d) * span
            wide[at : at + span, :] = piece(q, d).astype(F32).reshape(span, cw)
    gain_r = gr_ref[...]
    gain_i = gi_ref[...]
    for m in range(waves):
        real = wide[pl.ds(m, lat, stride=wave_rows), :].astype(BF16)
        imag = wide[pl.ds(waves + m, lat, stride=wave_rows), :].astype(BF16)
        leg = leg_ref[m]
        legt = legt_ref[m]
        cr = jnp.dot(leg, real, preferred_element_type=F32)
        ci = jnp.dot(leg, imag, preferred_element_type=F32)
        fr = (gain_r * cr - gain_i * ci).astype(BF16)
        fi = (gain_r * ci + gain_i * cr).astype(BF16)
        result[pl.ds(m, lat, stride=wave_rows), :] = jnp.dot(
            legt, fr, preferred_element_type=F32
        )
        result[pl.ds(waves + m, lat, stride=wave_rows), :] = jnp.dot(
            legt, fi, preferred_element_type=F32
        )
    for q in range(NQ):
        for d in range(nz):
            at = (q * nz + d) * span
            out_ref[d, q] = result[at : at + span, :].reshape(rows, wave_rows, cw).astype(BF16)


def first_of(shape, keep):
    block = (1,) * keep + shape[keep:]
    return pl.BlockSpec(block, lambda t: (0,) * len(shape))


def whole_of(array):
    shape = array.shape
    return pl.BlockSpec(shape, lambda t: (0,) * len(shape))


def legendre_step(own, others, leg, legt, gr, gi):
    nz = len(own)
    _, _, rows, wave_rows, cw = own[0].shape
    waves, degrees, lat = leg.shape
    specs = [first_of(own[0].shape, 2)] + [first_of(a.shape, 1) for a in own[1:]]
    return pl.pallas_call(
        functools.partial(legendre_kernel, nz),
        grid=(1,),
        in_specs=specs + [whole_of(a) for a in (*others, leg, legt, gr, gi)],
        out_specs=pl.BlockSpec((nz, NQ, rows, wave_rows, cw), lambda t: (0, 0, 0, 0, 0)),
        out_shape=jax.ShapeDtypeStruct((nz, NQ, rows, wave_rows, cw), BF16),
        scratch_shapes=[pltpu.VMEM((lat * wave_rows, cw), F32)] * 2,
        compiler_params=params(),
        cost_estimate=cost(
            8 * waves * degrees * lat * cw, 4 * lat * wave_rows * cw + 4 * leg.size
        ),
    )(*own, *others, leg, legt, gr, gi)


def inverse_kernel(nz, rows2, cw, lon_count, *refs):
    own = refs[:nz]
    others = refs[nz : nz + NQ - 1]
    upper_ref, lower_ref = refs[nz + NQ - 1 : nz + NQ + 1]
    outs = refs[nz + NQ + 1 : nz + NQ + 1 + lon_count]
    wide = refs[-1]
    wave_rows = own[0].shape[-2]
    cols = outs[0].shape[1]
    for t in range(rows2):
        for q in range(NQ):
            for d in range(nz):
                at = (q * nz + d) * wave_rows
                if q:
                    block = others[q - 1][d, t]
                elif d:
                    block = own[d][0, t]
                else:
                    block = own[0][0, 0, t]
                wide[t, at : at + wave_rows, :] = block.astype(F32)
    group = rows2 if cw % LANES == 0 else 1
    for first in range(0, rows2, group):
        x = [wide[first + i].astype(BF16) for i in range(group)]
        x = jnp.concatenate(x, axis=1) if group > 1 else x[0]
        acc = jnp.dot(upper_ref[...], x, preferred_element_type=F32)
        acc = acc + jnp.dot(lower_ref[...], x, preferred_element_type=F32)
        for i in range(group):
            for s in range(lon_count):
                outs[s][first + i] = acc[
                    s * cols : (s + 1) * cols, i * cw : (i + 1) * cw
                ].astype(BF16)


def inverse(own, others, upper, lower, lon_count):
    nz = len(own)
    _, _, rows, wave_rows, cw = own[0].shape
    rows2 = 2
    cols = upper.shape[0] // lon_count
    whole = pl.BlockSpec(upper.shape, lambda t: (0, 0))
    specs = [pl.BlockSpec((1, 1, rows2, wave_rows, cw), lambda t: (0, 0, t, 0, 0))]
    specs += [pl.BlockSpec((1, rows2, wave_rows, cw), lambda t: (0, t, 0, 0))] * (nz - 1)
    specs += [pl.BlockSpec((nz, rows2, wave_rows, cw), lambda t: (0, t, 0, 0))] * (NQ - 1)
    return pl.pallas_call(
        functools.partial(inverse_kernel, nz, rows2, cw, lon_count),
        grid=(rows // rows2,),
        in_specs=specs + [whole, whole],
        out_specs=[pl.BlockSpec((rows2, cols, cw), lambda t: (t, 0, 0))] * lon_count,
        out_shape=[jax.ShapeDtypeStruct((rows, cols, cw), BF16)] * lon_count,
        scratch_shapes=[pltpu.VMEM((rows2, nz * NQ * wave_rows, cw), F32)],
        compiler_params=params(),
        cost_estimate=cost(4 * upper.size * rows * cw, 4 * rows * cols * cw * lon_count),
    )(*own, *others, upper, lower)


def tail_kernel(lon_count, nch, slots, *refs):
    (place_ref, neighbour_ref, basis_ref, quad_ref) = refs[:4]
    count = lon_count * nch
    waves = refs[4 : 4 + count]
    lows = refs[4 + count : 4 + count + nch]
    highs = refs[4 + count + nch : 4 + count + 2 * nch]
    (
        disco_ref,
        gain_ref,
        w_in_ref,
        b_in_ref,
        w_out_ref,
        b_out_ref,
        field_ref,
        out_ref,
        spatial_ref,
        ring,
        conv_ref,
    ) = refs[4 + count + 2 * nch :]
    t = pl.program_id(0)
    rows = waves[0].shape[0]
    cols = field_ref.shape[1]
    cw = waves[0].shape[2]
    channels = field_ref.shape[2]

    def group(s, j):
        return place_ref[s] * nch + j

    def put(row, pick):
        for s in range(lon_count):
            for j in range(nch):
                ring[row, group(s, j)] = pick(s, j).astype(F32)

    @pl.when(t == 0)
    def _():
        for r in range(HALO):
            put(r, lambda s, j: lows[j][s, r])
            put(HALO + r, lambda s, j: waves[s * nch + j][r])

    @pl.when(t + HALO < rows)
    def _():
        put(t + 2 * HALO, lambda s, j: waves[s * nch + j][t + HALO])

    for r in range(HALO):

        @pl.when(t + HALO == rows + r)
        def _():
            put(rows + HALO + r, lambda s, j: highs[j][s, r])

    tile = 48 if cols % 48 == 0 else 8

    def one_group(g, carry):
        starts = []
        coefs = []
        for s in range(slots):
            n = neighbour_ref[t, s]
            starts.append((t + n // SPAN, n % SPAN))
            weight = disco_ref[g, pl.ds(basis_ref[t, s], 1), :]
            coefs.append(weight * quad_ref[t, s])

        def one_tile(i, carry):
            at = pl.multiple_of(i * tile, 8)
            acc = ring[t + HALO, g, pl.ds(at + HALO, tile), :]
            for (row, shift), coef in zip(starts, coefs):
                acc = acc + coef * ring[row, g, pl.ds(at + shift, tile), :]
            conv_ref[g, pl.ds(at, tile), :] = acc
            return carry

        return lax.fori_loop(0, cols // tile, one_tile, carry)

    lax.fori_loop(0, count, one_group, 0)
    spatial = jnp.concatenate([conv_ref[g] for g in range(count)], axis=1).astype(BF16)
    spatial_ref[0] = spatial
    tokens = spatial.astype(F32)
    center = jnp.mean(tokens, axis=1, keepdims=True)
    shifted = tokens - center
    spread = jnp.mean(shifted * shifted, axis=1, keepdims=True)
    normed = (shifted * lax.rsqrt(spread + 1e-05) * gain_ref[...]).astype(BF16)
    hidden = jnp.dot(normed, w_in_ref[...], preferred_element_type=F32) + b_in_ref[...]
    hidden = jax.nn.gelu(hidden).astype(BF16)
    result = jnp.dot(hidden, w_out_ref[...], preferred_element_type=F32)
    result = result + b_out_ref[...] + field_ref[0].astype(F32)
    out_ref[0] = result.astype(BF16)


def tail(place, neighbour, basis, quad, waves, lows, highs, disco, gain, w_in, b_in, w_out, b_out, field, lon_count, nch):
    rows, cols, channels = field.shape
    padded, cw = waves[0].shape[1:]
    count = lon_count * nch
    hidden = w_in.shape[1]
    row_spec = pl.BlockSpec((1, cols, channels), lambda t: (t, 0, 0))
    vm = [vmem_spec()]
    return pl.pallas_call(
        functools.partial(tail_kernel, lon_count, nch, neighbour.shape[1]),
        grid=(rows,),
        in_specs=[smem_spec()] * 4 + vm * (count + 2 * nch) + vm * 6 + [row_spec],
        out_specs=[row_spec, row_spec],
        out_shape=[jax.ShapeDtypeStruct(field.shape, BF16)] * 2,
        scratch_shapes=[
            pltpu.VMEM((rows + 2 * HALO, count, padded, cw), F32),
            pltpu.VMEM((count, cols, cw), F32),
        ],
        compiler_params=params(),
        cost_estimate=cost(
            4 * rows * cols * channels * hidden, 8 * field.size, rows * cols * hidden
        ),
    )(place, neighbour, basis, quad, *waves, *lows, *highs, disco, gain, w_in, b_in, w_out, b_out, field)


def swap(array, axis, mask):
    count = lax.axis_size(axis)
    return lax.ppermute(array, axis, [(i, i ^ mask) for i in range(count)])


def shards(
    field,
    quad_weight,
    legendre,
    filter_real,
    filter_imag,
    neighbour,
    basis,
    disco_quad,
    disco_weight,
    norm_gain,
    w_in,
    b_in,
    w_out,
    b_out,
):
    rows, cols, channels = field.shape
    lon_count = lax.axis_size("lon")
    lat_count = lax.axis_size("lat")
    nz = lat_count // NQ
    wave_block, degrees, nlat = legendre.shape
    wave_rows = 2 * wave_block
    mmax = wave_block * lat_count
    nlon = cols * lon_count
    cblock = channels // lon_count
    nch = max(1, cblock // LANES)
    cw = cblock // nch
    padded_cols = (cols + 2 * HALO + 7) // 8 * 8
    lat_id = lax.axis_index("lat")
    lon_id = lax.axis_index("lon")

    (fwd_u, fwd_l), (inv_u, inv_l) = tables_np(nlon, lon_count, wave_block, mmax, padded_cols)
    zq = np.arange(lat_count)
    qz = (zq % nz) * NQ + zq // nz

    def permutation(masks, width):
        source = (lat_id ^ jnp.asarray(masks, jnp.int32))[:, None] * width
        source = (source + jnp.arange(width, dtype=jnp.int32)[None, :]).reshape(-1)
        return (jnp.arange(lat_count * width, dtype=jnp.int32)[None, :] == source[:, None]).astype(BF16)

    perm_fwd = permutation(zq, wave_rows)
    perm_inv = permutation(qz, wave_rows)
    perm_lat = permutation(qz, rows)

    def forward_table(table):
        parts = [
            jnp.dot(
                perm_fwd,
                lax.dynamic_index_in_dim(jnp.asarray(table), lon_id ^ s, 0, keepdims=False),
                preferred_element_type=F32,
            )
            for s in range(lon_count)
        ]
        return jnp.concatenate(parts, axis=1).astype(BF16)

    def inverse_table(table):
        parts = [
            jnp.einsum(
                "kr,ur->ku",
                lax.dynamic_index_in_dim(jnp.asarray(table), lon_id ^ s, 0, keepdims=False),
                perm_inv,
                preferred_element_type=F32,
            )
            for s in range(lon_count)
        ]
        return jnp.concatenate(parts, axis=0).astype(BF16)

    fu, fl = forward_table(fwd_u), forward_table(fwd_l)
    iu, il = inverse_table(inv_u), inverse_table(inv_l)
    leg = jnp.einsum("mlt,ut->mlu", legendre, perm_lat, preferred_element_type=F32).astype(BF16)
    legt = jnp.einsum("mlt,ut->mul", legendre, perm_lat, preferred_element_type=F32).astype(BF16)

    def chunk_of(array, s, j):
        start = (lon_id ^ s) * cblock + j * cw
        return lax.dynamic_slice_in_dim(array, start, cw, array.ndim - 1)

    waves = [[None] * nch for _ in range(lon_count)]
    lows, highs = [], []
    received = [
        [swap(chunk_of(field, s, j), "lon", s) for s in range(1, lon_count)]
        for j in range(nch)
    ]
    for j in range(nch):
        blocks = [chunk_of(field, 0, j)] + received[j]
        spectrum = dft(blocks, quad_weight, fu, fl, nz, wave_rows)
        own = [spectrum] + [swap(spectrum[d], "lat", NQ * d) for d in range(1, nz)]

        def others_of(own):
            return [
                swap(
                    jnp.stack([own[0][0, q]] + [a[q] for a in own[1:]]), "lat", q
                )
                for q in range(1, NQ)
            ]

        gr = chunk_of(filter_real, 0, j)
        gi = chunk_of(filter_imag, 0, j)
        synthesis = legendre_step(own, others_of(own), leg, legt, gr, gi)
        own = [synthesis] + [swap(synthesis[d], "lat", NQ * d) for d in range(1, nz)]
        parts = inverse(own, others_of(own), iu, il, lon_count)
        waves[0][j] = parts[0]
        for s in range(1, lon_count):
            waves[s][j] = swap(parts[s], "lon", s)
    up = [(i, i + 1) for i in range(lat_count - 1)]
    down = [(i + 1, i) for i in range(lat_count - 1)]
    for j in range(nch):
        last = jnp.stack([waves[s][j][rows - HALO :] for s in range(lon_count)])
        first = jnp.stack([waves[s][j][:HALO] for s in range(lon_count)])
        lows.append(lax.ppermute(last, "lat", up))
        highs.append(lax.ppermute(first, "lat", down))

    place = (lon_id ^ jnp.arange(lon_count, dtype=jnp.int32)).astype(jnp.int32)
    disco = jnp.transpose(
        disco_weight.reshape(disco_weight.shape[0], lon_count * nch, cw), (1, 0, 2)
    )
    block_out, spatial = tail(
        place,
        neighbour,
        basis,
        disco_quad,
        [waves[s][j] for s in range(lon_count) for j in range(nch)],
        lows,
        highs,
        disco,
        norm_gain[None, :],
        w_in,
        b_in[None, :],
        w_out,
        b_out[None, :],
        field,
        lon_count,
        nch,
    )
    return (block_out, spatial)


def solution(mesh):
    grid = P("lat", "lon", None)
    rows = P("lat", None)
    placed = (grid, P("lat"), P("lat", None, None), P(), P(), rows, rows, rows) + (P(),) * 6
    return jax.shard_map(
        shards,
        mesh=mesh,
        in_specs=placed,
        out_specs=(grid, grid),
        check_vma=False,
    )
```

```python
import functools
import math

import jax
import jax.numpy as jnp
import ml_dtypes
import numpy as np
from jax import lax
from jax.experimental import pallas as pl
from jax.experimental.pallas import tpu as pltpu
from jax.sharding import PartitionSpec as P

HALO = 2
SPAN = 2 * HALO + 1
NQ = 4
LANES = 128
F32 = jnp.float32
BF16 = jnp.bfloat16
VMEM_LIMIT = 56 * 1024 * 1024


def vmem_spec():
    return pl.BlockSpec(memory_space=pltpu.VMEM)


def smem_spec():
    return pl.BlockSpec(memory_space=pltpu.SMEM)


def params():
    return pltpu.CompilerParams(
        vmem_limit_bytes=VMEM_LIMIT, dimension_semantics=("arbitrary",)
    )


def cost(flops, nbytes, trans=0):
    return pl.CostEstimate(
        flops=int(flops), bytes_accessed=int(nbytes), transcendentals=int(trans)
    )


def tables_np(nlon, lon_count, wave_block, mmax, padded_cols):
    blocks = mmax // wave_block
    waves = np.arange(mmax).reshape(blocks, 1, wave_block)
    waves = np.broadcast_to(waves, (blocks, 2, wave_block)).reshape(-1)
    imag = np.broadcast_to(np.arange(2).reshape(1, 2, 1), (blocks, 2, wave_block)).reshape(-1)

    def table(points):
        phase = (waves[:, None].astype(np.int64) * points[None, :]) % nlon
        angle = phase * (2.0 * math.pi / nlon)
        return np.where(imag[:, None] == 0, np.cos(angle), -np.sin(angle)) / math.sqrt(nlon)

    cols = nlon // lon_count
    fwd = np.stack([table(np.arange(cols) + b * cols) for b in range(lon_count)])
    factor = np.where(waves == 0, 1.0, 2.0)[:, None]
    inv = np.stack(
        [
            (factor * table((np.arange(padded_cols) - HALO + b * cols) % nlon)).T
            for b in range(lon_count)
        ]
    )
    return fwd.astype(ml_dtypes.bfloat16), inv.astype(ml_dtypes.bfloat16)


def any_spec():
    return pl.BlockSpec(memory_space=pl.ANY)


def step_rows(rows, limit):
    return max(r for r in range(1, limit + 1) if rows % r == 0)


def first_of(array, keep):
    block = (1,) * keep + array.shape[keep:]
    return pl.BlockSpec(block, lambda t: (0,) * array.ndim)


def whole_of(array):
    return pl.BlockSpec(array.shape, lambda t: (0,) * array.ndim)


def side_by_side(parts):
    return jnp.concatenate(parts, axis=1) if len(parts) > 1 else parts[0]


def dft_kernel(lon_count, nz, waits, quad_ref, *refs):
    blocks = refs[:lon_count]
    table_ref = refs[lon_count]
    outs = refs[lon_count + 1 + waits :]
    step = pl.program_id(0)
    rows, _, cw = blocks[0].shape
    wave_rows = outs[0].shape[2]
    group = rows if cw % LANES == 0 else 1
    for first in range(0, rows, group):
        x = [side_by_side([b[first + i] for i in range(group)]) for b in blocks]
        acc = jnp.dot(table_ref[...], jnp.concatenate(x, axis=0), preferred_element_type=F32)
        for i in range(group):
            t = first + i
            scaled = acc[:, i * cw : (i + 1) * cw] * quad_ref[step * rows + t]
            for d in range(nz):
                for q in range(NQ):
                    at = (d * NQ + q) * wave_rows
                    outs[d][q, t] = scaled[at : at + wave_rows].astype(BF16)


def dft(blocks, quad, table, nz, wave_rows, waits):
    rows, cols, cw = blocks[0].shape
    step = step_rows(rows, 6)
    lon_count = len(blocks)
    return pl.pallas_call(
        functools.partial(dft_kernel, lon_count, nz, len(waits)),
        grid=(rows // step,),
        in_specs=[smem_spec()]
        + [pl.BlockSpec((step, cols, cw), lambda t: (t, 0, 0))] * lon_count
        + [whole_of(table)]
        + [any_spec()] * len(waits),
        out_specs=[pl.BlockSpec((NQ, step, wave_rows, cw), lambda t: (0, t, 0, 0))] * nz,
        out_shape=[jax.ShapeDtypeStruct((NQ, rows, wave_rows, cw), BF16)] * nz,
        compiler_params=params(),
        cost_estimate=cost(2 * table.size * rows * cw, 8 * rows * cols * cw),
    )(quad, *blocks, table, *waits)


def legendre_kernel(nz, waits, *refs):
    own = refs[:nz]
    others = refs[nz : nz + NQ - 1]
    leg_ref, legt_ref, gr_ref, gi_ref = refs[nz + NQ - 1 : nz + NQ + 3]
    outs = refs[nz + NQ + 3 + waits : -2]
    wide, result = refs[-2:]
    waves, _, lat = leg_ref.shape
    _, rows, wave_rows, cw = outs[0].shape
    span = rows * wave_rows
    for q in range(NQ):
        for d in range(nz):
            at = (q * nz + d) * span
            piece = others[q - 1][d] if q else own[d][0]
            wide[at : at + span, :] = piece.astype(F32).reshape(span, cw)
    gain_r = gr_ref[...]
    gain_i = gi_ref[...]
    for m in range(waves):
        pair = [wide[pl.ds(r * waves + m, lat, stride=wave_rows), :] for r in range(2)]
        x = side_by_side(pair).astype(BF16)
        co = jnp.dot(leg_ref[m], x, preferred_element_type=F32)
        cr, ci = co[:, :cw], co[:, cw:]
        fr = gain_r * cr - gain_i * ci
        fi = gain_r * ci + gain_i * cr
        x = side_by_side([fr, fi]).astype(BF16)
        out = jnp.dot(legt_ref[m], x, preferred_element_type=F32)
        for r in range(2):
            result[pl.ds(r * waves + m, lat, stride=wave_rows), :] = out[:, r * cw : (r + 1) * cw]
    for q in range(NQ):
        for d in range(nz):
            at = (q * nz + d) * span
            outs[d][q] = result[at : at + span, :].reshape(rows, wave_rows, cw).astype(BF16)


def legendre_step(own, others, leg, legt, gr, gi, waits):
    nz = len(own)
    shape = own[0].shape
    _, rows, wave_rows, cw = shape
    waves, degrees, lat = leg.shape
    return pl.pallas_call(
        functools.partial(legendre_kernel, nz, len(waits)),
        grid=(1,),
        in_specs=[first_of(a, 1) for a in own]
        + [whole_of(a) for a in (*others, leg, legt, gr, gi)]
        + [any_spec()] * len(waits),
        out_specs=[pl.BlockSpec(shape, lambda t: (0, 0, 0, 0))] * nz,
        out_shape=[jax.ShapeDtypeStruct(shape, BF16)] * nz,
        scratch_shapes=[pltpu.VMEM((lat * wave_rows, cw), F32)] * 2,
        compiler_params=params(),
        cost_estimate=cost(
            8 * waves * degrees * lat * cw, 4 * lat * wave_rows * cw + 4 * leg.size
        ),
    )(*own, *others, leg, legt, gr, gi, *waits)


def inverse_kernel(nz, lon_count, *refs):
    own = refs[:nz]
    others = refs[nz : nz + NQ - 1]
    table_ref = refs[nz + NQ - 1]
    outs = refs[nz + NQ : nz + NQ + lon_count]
    wide = refs[-1]
    rows, _, cw = wide.shape
    wave_rows = own[0].shape[-2]
    cols = outs[0].shape[1]
    for t in range(rows):
        for q in range(NQ):
            for d in range(nz):
                at = (q * nz + d) * wave_rows
                block = others[q - 1][d, t] if q else own[d][0, t]
                wide[t, at : at + wave_rows, :] = block.astype(F32)
    group = rows if cw % LANES == 0 else 1
    for first in range(0, rows, group):
        x = side_by_side([wide[first + i].astype(BF16) for i in range(group)])
        acc = jnp.dot(table_ref[...], x, preferred_element_type=F32)
        for i in range(group):
            for s in range(lon_count):
                piece = acc[s * cols : (s + 1) * cols, i * cw : (i + 1) * cw]
                outs[s][first + i] = piece.astype(BF16)


def inverse(own, others, table, lon_count):
    nz = len(own)
    _, rows, wave_rows, cw = own[0].shape
    step = step_rows(rows, 6)
    cols = table.shape[0] // lon_count
    specs = [pl.BlockSpec((1, step, wave_rows, cw), lambda t: (0, t, 0, 0))] * nz
    specs += [pl.BlockSpec((nz, step, wave_rows, cw), lambda t: (0, t, 0, 0))] * (NQ - 1)
    return pl.pallas_call(
        functools.partial(inverse_kernel, nz, lon_count),
        grid=(rows // step,),
        in_specs=specs + [whole_of(table)],
        out_specs=[pl.BlockSpec((step, cols, cw), lambda t: (t, 0, 0))] * lon_count,
        out_shape=[jax.ShapeDtypeStruct((rows, cols, cw), BF16)] * lon_count,
        scratch_shapes=[pltpu.VMEM((step, nz * NQ * wave_rows, cw), F32)],
        compiler_params=params(),
        cost_estimate=cost(2 * table.size * rows * cw, 4 * rows * cols * cw * lon_count),
    )(*own, *others, table)


def window_kernel(cols, place_ref, neighbour_ref, basis_ref, quad_ref, wave_ref, low_ref, high_ref, disco_ref, out_ref, ring):
    step = pl.program_id(0)
    rows = wave_ref.shape[0]
    slots = neighbour_ref.shape[1]
    per_step = out_ref.shape[0]
    group = place_ref[0]

    @pl.when(step == 0)
    def _():
        for r in range(HALO):
            ring[r] = low_ref[r].astype(F32)
            ring[HALO + r] = wave_ref[r].astype(F32)
            ring[rows + HALO + r] = high_ref[r].astype(F32)

    for i in range(per_step):
        t = step * per_step + i

        @pl.when(t + HALO < rows)
        def _(t=t):
            ring[t + 2 * HALO] = wave_ref[t + HALO].astype(F32)

    tile = 48 if cols % 48 == 0 else 8
    for i in range(per_step):
        t = step * per_step + i
        taps = []
        for s in range(slots):
            n = neighbour_ref[t, s]
            weight = disco_ref[group, pl.ds(basis_ref[t, s], 1), :]
            taps.append((t + n // SPAN, n % SPAN, weight * quad_ref[t, s]))
        for at in range(0, cols, tile):
            acc = ring[t + HALO, pl.ds(at + HALO, tile), :]
            for row, shift, coef in taps:
                acc = acc + coef * ring[row, pl.ds(at + shift, tile), :]
            out_ref[i, pl.ds(at, tile), :] = acc.astype(BF16)


def window(place, neighbour, basis, quad, wave, low, high, disco, cols):
    rows, padded, cw = wave.shape
    per_step = step_rows(rows, 2)
    return pl.pallas_call(
        functools.partial(window_kernel, cols),
        grid=(rows // per_step,),
        in_specs=[smem_spec()] * 4 + [whole_of(a) for a in (wave, low, high, disco)],
        out_specs=pl.BlockSpec((per_step, cols, cw), lambda t: (t, 0, 0)),
        out_shape=jax.ShapeDtypeStruct((rows, cols, cw), BF16),
        scratch_shapes=[pltpu.VMEM((rows + 2 * HALO, padded, cw), F32)],
        compiler_params=params(),
        cost_estimate=cost(8 * rows * cols * cw * 24, 4 * rows * cols * cw),
    )(place, neighbour, basis, quad, wave, low, high, disco)


def mlp_kernel(place_ref, *refs):
    count = len(refs) - 9
    groups = refs[:count]
    gain_ref, w_in_ref, b_in_ref, w_out_ref, b_out_ref, field_ref, out_ref, spatial_ref, ordered = refs[count:]
    per_step, cols, cw = groups[0].shape
    for k in range(count):
        ordered[place_ref[k]] = groups[k][...].reshape(per_step * cols, cw)
    spatial = jnp.concatenate([ordered[k] for k in range(count)], axis=1)
    spatial_ref[...] = spatial.reshape(spatial_ref.shape)
    tokens = spatial.astype(F32)
    center = jnp.mean(tokens, axis=1, keepdims=True)
    shifted = tokens - center
    spread = jnp.mean(shifted * shifted, axis=1, keepdims=True)
    normed = (shifted * lax.rsqrt(spread + 1e-05) * gain_ref[...]).astype(BF16)
    hidden = jnp.dot(normed, w_in_ref[...], preferred_element_type=F32) + b_in_ref[...]
    hidden = jax.nn.gelu(hidden).astype(BF16)
    result = jnp.dot(hidden, w_out_ref[...], preferred_element_type=F32)
    result = result + b_out_ref[...] + field_ref[...].reshape(tokens.shape).astype(F32)
    out_ref[...] = result.astype(BF16).reshape(out_ref.shape)


def mlp(place, groups, gain, w_in, b_in, w_out, b_out, field):
    rows, cols, channels = field.shape
    cw = groups[0].shape[2]
    per_step = step_rows(rows, 2)
    block = pl.BlockSpec((per_step, cols, channels), lambda t: (t, 0, 0))
    part = pl.BlockSpec((per_step, cols, cw), lambda t: (t, 0, 0))
    return pl.pallas_call(
        mlp_kernel,
        grid=(rows // per_step,),
        in_specs=[smem_spec()]
        + [part] * len(groups)
        + [whole_of(a) for a in (gain, w_in, b_in, w_out, b_out)]
        + [block],
        out_specs=[block, block],
        out_shape=[jax.ShapeDtypeStruct(field.shape, BF16)] * 2,
        scratch_shapes=[pltpu.VMEM((len(groups), per_step * cols, cw), BF16)],
        compiler_params=params(),
        cost_estimate=cost(
            4 * field.size * w_in.shape[1], 8 * field.size, rows * cols * w_in.shape[1]
        ),
    )(place, *groups, gain, w_in, b_in, w_out, b_out, field)


def swap(array, axis, mask):
    count = lax.axis_size(axis)
    return lax.ppermute(array, axis, [(i, i ^ mask) for i in range(count)])


def shards(
    field,
    quad_weight,
    legendre,
    filter_real,
    filter_imag,
    neighbour,
    basis,
    disco_quad,
    disco_weight,
    norm_gain,
    w_in,
    b_in,
    w_out,
    b_out,
):
    rows, cols, channels = field.shape
    lon_count = lax.axis_size("lon")
    lat_count = lax.axis_size("lat")
    nz = lat_count // NQ
    wave_block, degrees, nlat = legendre.shape
    wave_rows = 2 * wave_block
    mmax = wave_block * lat_count
    nlon = cols * lon_count
    cblock = channels // lon_count
    nch = max(1, cblock // LANES)
    cw = cblock // nch
    padded_cols = (cols + 2 * HALO + 7) // 8 * 8
    lat_id = lax.axis_index("lat")
    lon_id = lax.axis_index("lon")

    fwd, inv = tables_np(nlon, lon_count, wave_block, mmax, padded_cols)
    zq = np.arange(lat_count)
    qz = (zq % nz) * NQ + zq // nz

    def permutation(masks, width):
        source = (lat_id ^ jnp.asarray(masks, jnp.int32))[:, None] * width
        source = (source + jnp.arange(width, dtype=jnp.int32)[None, :]).reshape(-1)
        return (jnp.arange(lat_count * width, dtype=jnp.int32)[None, :] == source[:, None]).astype(BF16)

    perm_fwd = permutation(zq, wave_rows)
    perm_inv = permutation(qz, wave_rows)
    perm_lat = permutation(qz, rows)

    def forward_table(table):
        parts = [
            jnp.dot(
                perm_fwd,
                lax.dynamic_index_in_dim(jnp.asarray(table), lon_id ^ s, 0, keepdims=False),
                preferred_element_type=F32,
            )
            for s in range(lon_count)
        ]
        return jnp.concatenate(parts, axis=1).astype(BF16)

    def inverse_table(table):
        parts = [
            jnp.einsum(
                "kr,ur->ku",
                lax.dynamic_index_in_dim(jnp.asarray(table), lon_id ^ s, 0, keepdims=False),
                perm_inv,
                preferred_element_type=F32,
            )
            for s in range(lon_count)
        ]
        return jnp.concatenate(parts, axis=0).astype(BF16)

    fwd = forward_table(fwd)
    inv = inverse_table(inv)
    leg = jnp.einsum("mlt,ut->mlu", legendre, perm_lat, preferred_element_type=F32).astype(BF16)
    legt = jnp.einsum("mlt,ut->mul", legendre, perm_lat, preferred_element_type=F32).astype(BF16)

    def chunk_of(array, s, j):
        start = (lon_id ^ s) * cblock + j * cw
        return lax.dynamic_slice_in_dim(array, start, cw, array.ndim - 1)

    def across(own):
        return [swap(jnp.stack([a[q] for a in own]), "lat", q) for q in range(1, NQ)]

    def along(arrays):
        return [arrays[0]] + [swap(arrays[d], "lat", NQ * d) for d in range(1, nz)]

    disco = disco_weight.reshape(disco_weight.shape[0], lon_count * nch, cw)
    disco = jnp.transpose(disco, (1, 0, 2))
    up = [(i, i + 1) for i in range(lat_count - 1)]
    down = [(i + 1, i) for i in range(lat_count - 1)]

    def convolved(wave, s, j):
        low = lax.ppermute(wave[rows - HALO :], "lat", up)
        high = lax.ppermute(wave[:HALO], "lat", down)
        place = ((lon_id ^ s) * nch + j).astype(jnp.int32)
        done = window(
            place[None], neighbour, basis, disco_quad, wave, low, high, disco, cols
        )
        return place, done

    received = [
        [swap(chunk_of(field, s, j), "lon", s) for s in range(1, lon_count)]
        for j in range(nch)
    ]
    spectra, waits = [], []
    for j in range(nch):
        blocks = [chunk_of(field, 0, j)] + received[j]
        spectra.append(along(dft(blocks, quad_weight, fwd, nz, wave_rows, waits)))
        waits = [spectra[-1][1]]
    synthesis, waits = [], []
    for j in range(nch):
        gr = chunk_of(filter_real, 0, j)
        gi = chunk_of(filter_imag, 0, j)
        full = legendre_step(spectra[j], across(spectra[j]), leg, legt, gr, gi, waits)
        synthesis.append(along(full))
        waits = [full[0]]
    groups = []
    for j in range(nch):
        parts = inverse(synthesis[j], across(synthesis[j]), inv, lon_count)
        for s in range(lon_count):
            wave = swap(parts[s], "lon", s) if s else parts[0]
            groups.append(convolved(wave, s, j))
    block_out, spatial = mlp(
        jnp.stack([place for place, _ in groups]),
        [done for _, done in groups],
        norm_gain[None, :],
        w_in,
        b_in[None, :],
        w_out,
        b_out[None, :],
        field,
    )
    return (block_out, spatial)


def solution(mesh):
    grid = P("lat", "lon", None)
    rows = P("lat", None)
    placed = (grid, P("lat"), P("lat", None, None), P(), P(), rows, rows, rows) + (P(),) * 6
    return jax.shard_map(
        shards,
        mesh=mesh,
        in_specs=placed,
        out_specs=(grid, grid),
        check_vma=False,
    )
```

```python
import functools
import math

import jax
import jax.numpy as jnp
import ml_dtypes
import numpy as np
from jax import lax
from jax.experimental import pallas as pl
from jax.experimental.pallas import tpu as pltpu
from jax.sharding import PartitionSpec as P

HALO = 2
SPAN = 2 * HALO + 1
NQ = 4
LANES = 128
F32 = jnp.float32
BF16 = jnp.bfloat16
VMEM_LIMIT = 56 * 1024 * 1024


def vmem_spec():
    return pl.BlockSpec(memory_space=pltpu.VMEM)


def smem_spec():
    return pl.BlockSpec(memory_space=pltpu.SMEM)


def params():
    return pltpu.CompilerParams(
        vmem_limit_bytes=VMEM_LIMIT, dimension_semantics=("arbitrary",)
    )


def cost(flops, nbytes, trans=0):
    return pl.CostEstimate(
        flops=int(flops), bytes_accessed=int(nbytes), transcendentals=int(trans)
    )


def tables_np(nlon, lon_count, wave_block, mmax, padded_cols):
    blocks = mmax // wave_block
    waves = np.arange(mmax).reshape(blocks, 1, wave_block)
    waves = np.broadcast_to(waves, (blocks, 2, wave_block)).reshape(-1)
    imag = np.broadcast_to(np.arange(2).reshape(1, 2, 1), (blocks, 2, wave_block)).reshape(-1)

    def table(points):
        phase = (waves[:, None].astype(np.int64) * points[None, :]) % nlon
        angle = phase * (2.0 * math.pi / nlon)
        return np.where(imag[:, None] == 0, np.cos(angle), -np.sin(angle)) / math.sqrt(nlon)

    cols = nlon // lon_count
    fwd = np.stack([table(np.arange(cols) + b * cols) for b in range(lon_count)])
    factor = np.where(waves == 0, 1.0, 2.0)[:, None]
    inv = np.stack(
        [
            (factor * table((np.arange(padded_cols) - HALO + b * cols) % nlon)).T
            for b in range(lon_count)
        ]
    )
    return fwd.astype(ml_dtypes.bfloat16), inv.astype(ml_dtypes.bfloat16)


def any_spec():
    return pl.BlockSpec(memory_space=pl.ANY)


def step_rows(rows, limit):
    return max(r for r in range(1, limit + 1) if rows % r == 0)


def first_of(array, keep):
    block = (1,) * keep + array.shape[keep:]
    return pl.BlockSpec(block, lambda t: (0,) * array.ndim)


def whole_of(array):
    return pl.BlockSpec(array.shape, lambda t: (0,) * array.ndim)


def side_by_side(parts):
    return jnp.concatenate(parts, axis=1) if len(parts) > 1 else parts[0]


def lane_blocks(cw):
    return cw % LANES == 0


def pick_kernel(index_ref, field_ref, *refs):
    refs[-1][...] = field_ref[...]


def pick(array, index, cw, waits):
    if not lane_blocks(cw):
        return lax.dynamic_slice_in_dim(array, index * cw, cw, array.ndim - 1)
    rows, cols, _ = array.shape
    step = step_rows(rows, 6)
    return pl.pallas_call(
        pick_kernel,
        grid_spec=pltpu.PrefetchScalarGridSpec(
            num_scalar_prefetch=1,
            grid=(rows // step,),
            in_specs=[pl.BlockSpec((step, cols, cw), lambda t, i: (t, 0, i[0]))]
            + [any_spec()] * len(waits),
            out_specs=pl.BlockSpec((step, cols, cw), lambda t, i: (t, 0, 0)),
        ),
        out_shape=jax.ShapeDtypeStruct((rows, cols, cw), array.dtype),
        compiler_params=params(),
        cost_estimate=cost(0, 4 * rows * cols * cw),
    )(index[None], array, *waits)


def rows_kernel(count, wave_ref, *refs):
    first_ref, last_ref = refs[-2:]
    rows = wave_ref.shape[0]
    for r in range(HALO):
        first_ref[r] = wave_ref[r]
        last_ref[r] = wave_ref[rows - HALO + r]


def edge_rows(wave, waits):
    edge = jax.ShapeDtypeStruct((HALO,) + wave.shape[1:], wave.dtype)
    return pl.pallas_call(
        functools.partial(rows_kernel, len(waits)),
        in_specs=[vmem_spec()] + [any_spec()] * len(waits),
        out_specs=[vmem_spec()] * 2,
        out_shape=[edge, edge],
        compiler_params=pltpu.CompilerParams(vmem_limit_bytes=VMEM_LIMIT),
        cost_estimate=cost(0, 8 * edge.size),
    )(wave, *waits)


def dft_kernel(lon_count, nz, waits, index_ref, quad_ref, *refs):
    blocks = refs[:lon_count]
    table_ref = refs[lon_count]
    outs = refs[lon_count + 1 + waits :]
    step = pl.program_id(0)
    rows, _, cw = blocks[0].shape
    wave_rows = outs[0].shape[2]
    group = rows if cw % LANES == 0 else 1
    for first in range(0, rows, group):
        x = [side_by_side([b[first + i] for i in range(group)]) for b in blocks]
        acc = jnp.dot(table_ref[...], jnp.concatenate(x, axis=0), preferred_element_type=F32)
        for i in range(group):
            t = first + i
            scaled = acc[:, i * cw : (i + 1) * cw] * quad_ref[step * rows + t]
            for d in range(nz):
                for q in range(NQ):
                    at = (d * NQ + q) * wave_rows
                    outs[d][q, t] = scaled[at : at + wave_rows].astype(BF16)


def dft(field, index, received, quad, table, nz, wave_rows, cw, waits):
    rows, cols, _ = field.shape
    step = step_rows(rows, 6)
    lon_count = 1 + len(received)
    own = pl.BlockSpec((step, cols, cw), lambda t, i: (t, 0, i[0]))
    if not lane_blocks(cw):
        field = pick(field, index, cw, [])
        own = pl.BlockSpec((step, cols, cw), lambda t, i: (t, 0, 0))
    return pl.pallas_call(
        functools.partial(dft_kernel, lon_count, nz, len(waits)),
        grid_spec=pltpu.PrefetchScalarGridSpec(
            num_scalar_prefetch=1,
            grid=(rows // step,),
            in_specs=[smem_spec(), own]
            + [pl.BlockSpec((step, cols, cw), lambda t, i: (t, 0, 0))] * len(received)
            + [pl.BlockSpec(table.shape, lambda t, i: (0, 0))]
            + [any_spec()] * len(waits),
            out_specs=[
                pl.BlockSpec((NQ, step, wave_rows, cw), lambda t, i: (0, t, 0, 0))
            ]
            * nz,
        ),
        out_shape=[jax.ShapeDtypeStruct((NQ, rows, wave_rows, cw), BF16)] * nz,
        compiler_params=params(),
        cost_estimate=cost(2 * table.size * rows * cw, 8 * rows * cols * cw),
    )(index[None], quad, field, *received, table, *waits)


def regroup_kernel(count, outs, *refs):
    sources = refs[:count]
    for k, out_ref in enumerate(refs[-outs:]):
        for i, ref in enumerate(sources):
            out_ref[i] = ref[k + 1]


def regroup(arrays, waits):
    count = len(arrays)
    outs = arrays[0].shape[0] - 1
    shape = (count,) + arrays[0].shape[1:]
    return pl.pallas_call(
        functools.partial(regroup_kernel, count, outs),
        grid=(1,),
        in_specs=[whole_of(a) for a in arrays] + [any_spec()] * len(waits),
        out_specs=[pl.BlockSpec(shape, lambda t: (0,) * len(shape))] * outs,
        out_shape=[jax.ShapeDtypeStruct(shape, BF16)] * outs,
        compiler_params=params(),
        cost_estimate=cost(0, 4 * outs * math.prod(shape)),
    )(*arrays, *waits)


def legendre_kernel(nz, waits, *refs):
    own = refs[:nz]
    others = refs[nz : nz + NQ - 1]
    leg_ref, legt_ref, gr_ref, gi_ref = refs[nz + NQ - 1 : nz + NQ + 3]
    outs = refs[nz + NQ + 3 + waits : -2]
    wide, result = refs[-2:]
    waves, _, lat = leg_ref.shape
    _, rows, wave_rows, cw = outs[0].shape
    span = rows * wave_rows
    for q in range(NQ):
        for d in range(nz):
            at = (q * nz + d) * span
            piece = others[q - 1][d] if q else own[d][0]
            wide[at : at + span, :] = piece.astype(F32).reshape(span, cw)
    gain_r = gr_ref[...]
    gain_i = gi_ref[...]
    for m in range(waves):
        pair = [wide[pl.ds(r * waves + m, lat, stride=wave_rows), :] for r in range(2)]
        x = side_by_side(pair).astype(BF16)
        co = jnp.dot(leg_ref[m], x, preferred_element_type=F32)
        cr, ci = co[:, :cw], co[:, cw:]
        fr = gain_r * cr - gain_i * ci
        fi = gain_r * ci + gain_i * cr
        x = side_by_side([fr, fi]).astype(BF16)
        out = jnp.dot(legt_ref[m], x, preferred_element_type=F32)
        for r in range(2):
            result[pl.ds(r * waves + m, lat, stride=wave_rows), :] = out[:, r * cw : (r + 1) * cw]
    for q in range(NQ):
        for d in range(nz):
            at = (q * nz + d) * span
            outs[q][d] = result[at : at + span, :].reshape(rows, wave_rows, cw).astype(BF16)


def legendre_step(own, others, leg, legt, gr, gi, waits):
    nz = len(own)
    _, rows, wave_rows, cw = own[0].shape
    shape = (nz, rows, wave_rows, cw)
    waves, degrees, lat = leg.shape
    return pl.pallas_call(
        functools.partial(legendre_kernel, nz, len(waits)),
        grid=(1,),
        in_specs=[first_of(a, 1) for a in own]
        + [whole_of(a) for a in (*others, leg, legt, gr, gi)]
        + [any_spec()] * len(waits),
        out_specs=[pl.BlockSpec(shape, lambda t: (0, 0, 0, 0))] * NQ,
        out_shape=[jax.ShapeDtypeStruct(shape, BF16)] * NQ,
        scratch_shapes=[pltpu.VMEM((lat * wave_rows, cw), F32)] * 2,
        compiler_params=params(),
        cost_estimate=cost(0, 14000000),
    )(*own, *others, leg, legt, gr, gi, *waits)


def inverse_kernel(nz, lon_count, *refs):
    near = refs[:NQ]
    far = refs[NQ : NQ + nz - 1]
    table_ref = refs[NQ + nz - 1]
    outs = refs[NQ + nz : NQ + nz + lon_count]
    wide = refs[-1]
    rows, _, cw = wide.shape
    wave_rows = near[0].shape[-2]
    cols = outs[0].shape[1]
    for t in range(rows):
        for q in range(NQ):
            for d in range(nz):
                at = (q * nz + d) * wave_rows
                block = far[d - 1][q, t] if d else near[q][0, t]
                wide[t, at : at + wave_rows, :] = block.astype(F32)
    group = rows if cw % LANES == 0 else 1
    for first in range(0, rows, group):
        x = side_by_side([wide[first + i].astype(BF16) for i in range(group)])
        acc = jnp.dot(table_ref[...], x, preferred_element_type=F32)
        for i in range(group):
            for s in range(lon_count):
                piece = acc[s * cols : (s + 1) * cols, i * cw : (i + 1) * cw]
                outs[s][first + i] = piece.astype(BF16)


def inverse(near, far, table, lon_count):
    nz = len(far) + 1
    _, rows, wave_rows, cw = near[0].shape
    step = step_rows(rows, 6)
    cols = table.shape[0] // lon_count
    specs = [pl.BlockSpec((1, step, wave_rows, cw), lambda t: (0, t, 0, 0))] * NQ
    specs += [pl.BlockSpec((NQ, step, wave_rows, cw), lambda t: (0, t, 0, 0))] * (nz - 1)
    return pl.pallas_call(
        functools.partial(inverse_kernel, nz, lon_count),
        grid=(rows // step,),
        in_specs=specs + [whole_of(table)],
        out_specs=[pl.BlockSpec((step, cols, cw), lambda t: (t, 0, 0))] * lon_count,
        out_shape=[jax.ShapeDtypeStruct((rows, cols, cw), BF16)] * lon_count,
        scratch_shapes=[pltpu.VMEM((step, nz * NQ * wave_rows, cw), F32)],
        compiler_params=params(),
        cost_estimate=cost(0, 14000000),
    )(*near, *far, table)


def window_kernel(cols, place_ref, neighbour_ref, basis_ref, quad_ref, wave_ref, low_ref, high_ref, disco_ref, out_ref, ring):
    step = pl.program_id(0)
    rows = wave_ref.shape[0]
    slots = neighbour_ref.shape[1]
    per_step = out_ref.shape[0]
    group = place_ref[0]

    @pl.when(step == 0)
    def _():
        for r in range(HALO):
            ring[r] = low_ref[r].astype(F32)
            ring[HALO + r] = wave_ref[r].astype(F32)
            ring[rows + HALO + r] = high_ref[r].astype(F32)

    for i in range(per_step):
        t = step * per_step + i

        @pl.when(t + HALO < rows)
        def _(t=t):
            ring[t + 2 * HALO] = wave_ref[t + HALO].astype(F32)

    tile = 48 if cols % 48 == 0 else 8
    for i in range(per_step):
        t = step * per_step + i
        taps = []
        for s in range(slots):
            n = neighbour_ref[t, s]
            weight = disco_ref[group, pl.ds(basis_ref[t, s], 1), :]
            taps.append((t + n // SPAN, n % SPAN, weight * quad_ref[t, s]))
        for at in range(0, cols, tile):
            acc = ring[t + HALO, pl.ds(at + HALO, tile), :]
            for row, shift, coef in taps:
                acc = acc + coef * ring[row, pl.ds(at + shift, tile), :]
            out_ref[i, pl.ds(at, tile), :] = acc.astype(BF16)


def window(place, neighbour, basis, quad, wave, low, high, disco, cols):
    rows, padded, cw = wave.shape
    per_step = step_rows(rows, 2)
    return pl.pallas_call(
        functools.partial(window_kernel, cols),
        grid=(rows // per_step,),
        in_specs=[smem_spec()] * 4 + [whole_of(a) for a in (wave, low, high, disco)],
        out_specs=pl.BlockSpec((per_step, cols, cw), lambda t: (t, 0, 0)),
        out_shape=jax.ShapeDtypeStruct((rows, cols, cw), BF16),
        scratch_shapes=[pltpu.VMEM((rows + 2 * HALO, padded, cw), F32)],
        compiler_params=params(),
        cost_estimate=cost(0, 20000000),
    )(place, neighbour, basis, quad, wave, low, high, disco)


def mlp_kernel(place_ref, *refs):
    count = len(refs) - 9
    groups = refs[:count]
    gain_ref, w_in_ref, b_in_ref, w_out_ref, b_out_ref, field_ref, out_ref, spatial_ref, ordered = refs[count:]
    per_step, cols, cw = groups[0].shape
    for k in range(count):
        ordered[place_ref[k]] = groups[k][...].reshape(per_step * cols, cw)
    spatial = jnp.concatenate([ordered[k] for k in range(count)], axis=1)
    spatial_ref[...] = spatial.reshape(spatial_ref.shape)
    tokens = spatial.astype(F32)
    center = jnp.mean(tokens, axis=1, keepdims=True)
    shifted = tokens - center
    spread = jnp.mean(shifted * shifted, axis=1, keepdims=True)
    normed = (shifted * lax.rsqrt(spread + 1e-05) * gain_ref[...]).astype(BF16)
    hidden = jnp.dot(normed, w_in_ref[...], preferred_element_type=F32) + b_in_ref[...]
    hidden = jax.nn.gelu(hidden).astype(BF16)
    result = jnp.dot(hidden, w_out_ref[...], preferred_element_type=F32)
    result = result + b_out_ref[...] + field_ref[...].reshape(tokens.shape).astype(F32)
    out_ref[...] = result.astype(BF16).reshape(out_ref.shape)


def mlp(place, groups, gain, w_in, b_in, w_out, b_out, field):
    rows, cols, channels = field.shape
    cw = groups[0].shape[2]
    per_step = step_rows(rows, 2)
    block = pl.BlockSpec((per_step, cols, channels), lambda t: (t, 0, 0))
    part = pl.BlockSpec((per_step, cols, cw), lambda t: (t, 0, 0))
    return pl.pallas_call(
        mlp_kernel,
        grid=(rows // per_step,),
        in_specs=[smem_spec()]
        + [part] * len(groups)
        + [whole_of(a) for a in (gain, w_in, b_in, w_out, b_out)]
        + [block],
        out_specs=[block, block],
        out_shape=[jax.ShapeDtypeStruct(field.shape, BF16)] * 2,
        scratch_shapes=[pltpu.VMEM((len(groups), per_step * cols, cw), BF16)],
        compiler_params=params(),
        cost_estimate=cost(
            4 * field.size * w_in.shape[1], 8 * field.size, rows * cols * w_in.shape[1]
        ),
    )(place, *groups, gain, w_in, b_in, w_out, b_out, field)


def swap(array, axis, mask):
    count = lax.axis_size(axis)
    return lax.ppermute(array, axis, [(i, i ^ mask) for i in range(count)])


def shards(
    field,
    quad_weight,
    legendre,
    filter_real,
    filter_imag,
    neighbour,
    basis,
    disco_quad,
    disco_weight,
    norm_gain,
    w_in,
    b_in,
    w_out,
    b_out,
):
    rows, cols, channels = field.shape
    lon_count = lax.axis_size("lon")
    lat_count = lax.axis_size("lat")
    nz = lat_count // NQ
    wave_block, degrees, nlat = legendre.shape
    wave_rows = 2 * wave_block
    mmax = wave_block * lat_count
    nlon = cols * lon_count
    cblock = channels // lon_count
    nch = max(1, cblock // LANES)
    cw = cblock // nch
    padded_cols = (cols + 2 * HALO + 7) // 8 * 8
    lat_id = lax.axis_index("lat")
    lon_id = lax.axis_index("lon")

    fwd, inv = tables_np(nlon, lon_count, wave_block, mmax, padded_cols)
    zq = np.arange(lat_count)
    qz = (zq % nz) * NQ + zq // nz

    def permutation(masks, width):
        source = (lat_id ^ jnp.asarray(masks, jnp.int32))[:, None] * width
        source = (source + jnp.arange(width, dtype=jnp.int32)[None, :]).reshape(-1)
        return (jnp.arange(lat_count * width, dtype=jnp.int32)[None, :] == source[:, None]).astype(BF16)

    perm_fwd = permutation(zq, wave_rows)
    perm_inv = permutation(qz, wave_rows)
    perm_lat = permutation(qz, rows)

    def forward_table(table):
        parts = [
            jnp.dot(
                perm_fwd,
                lax.dynamic_index_in_dim(jnp.asarray(table), lon_id ^ s, 0, keepdims=False),
                preferred_element_type=F32,
            )
            for s in range(lon_count)
        ]
        return jnp.concatenate(parts, axis=1).astype(BF16)

    def inverse_table(table):
        parts = [
            jnp.einsum(
                "kr,ur->ku",
                lax.dynamic_index_in_dim(jnp.asarray(table), lon_id ^ s, 0, keepdims=False),
                perm_inv,
                preferred_element_type=F32,
            )
            for s in range(lon_count)
        ]
        return jnp.concatenate(parts, axis=0).astype(BF16)

    fwd = forward_table(fwd)
    inv = inverse_table(inv)
    leg = jnp.einsum("mlt,ut->mlu", legendre, perm_lat, preferred_element_type=F32).astype(BF16)
    legt = jnp.einsum("mlt,ut->mul", legendre, perm_lat, preferred_element_type=F32).astype(BF16)

    def chunk_of(array, s, j):
        start = (lon_id ^ s) * cblock + j * cw
        return lax.dynamic_slice_in_dim(array, start, cw, array.ndim - 1)

    def along(blocks):
        return [swap(block, "lat", NQ * (d + 1)) for d, block in enumerate(blocks)]

    def across(blocks):
        return [swap(block, "lat", q + 1) for q, block in enumerate(blocks)]

    disco = disco_weight.reshape(disco_weight.shape[0], lon_count * nch, cw)
    disco = jnp.transpose(disco, (1, 0, 2))
    up = [(i, i + 1) for i in range(lat_count - 1)]
    down = [(i + 1, i) for i in range(lat_count - 1)]

    def convolved(wave, s, j, waits):
        first, last = edge_rows(wave, waits)
        low = lax.ppermute(last, "lat", up)
        high = lax.ppermute(first, "lat", down)
        place = ((lon_id ^ s) * nch + j).astype(jnp.int32)
        done = window(
            place[None], neighbour, basis, disco_quad, wave, low, high, disco, cols
        )
        return place, done

    def channel_index(s, j):
        return ((lon_id ^ s) * nch + j).astype(jnp.int32)

    received, waits = [], []
    for j in range(nch):
        received.append(
            [
                swap(pick(field, channel_index(s, j), cw, waits), "lon", s)
                for s in range(1, lon_count)
            ]
        )
        waits = [fwd]
    spectra, waits = [], []
    for j in range(nch):
        arrays = dft(
            field, channel_index(0, j), received[j], quad_weight, fwd, nz, wave_rows, cw, waits
        )
        spectra.append([arrays[0]] + along(arrays[1:]))
        waits = [spectra[-1][1]]
        latest = arrays[0]
    near = []
    waits = [latest]
    for j in range(nch):
        gr = chunk_of(filter_real, 0, j)
        gi = chunk_of(filter_imag, 0, j)
        full = legendre_step(
            spectra[j], across(regroup(spectra[j], waits)), leg, legt, gr, gi, []
        )
        near.append([full[0]] + across(full[1:]))
        waits = []
    parts = []
    for j in range(nch):
        parts.append(inverse(near[j], along(regroup(near[j], [])), inv, lon_count))
    groups = [convolved(parts[j][0], 0, j, []) for j in range(nch)]
    for j in range(nch):
        waits = [done for _, done in groups] if j == nch - 1 else []
        for s in range(1, lon_count):
            groups.append(convolved(swap(parts[j][s], "lon", s), s, j, waits))
    block_out, spatial = mlp(
        jnp.stack([place for place, _ in groups]),
        [done for _, done in groups],
        norm_gain[None, :],
        w_in,
        b_in[None, :],
        w_out,
        b_out[None, :],
        field,
    )
    return (block_out, spatial)


def solution(mesh):
    grid = P("lat", "lon", None)
    rows = P("lat", None)
    placed = (grid, P("lat"), P("lat", None, None), P(), P(), rows, rows, rows) + (P(),) * 6
    return jax.shard_map(
        shards,
        mesh=mesh,
        in_specs=placed,
        out_specs=(grid, grid),
        check_vma=False,
    )
```

```python
import functools
import math

import jax
import jax.numpy as jnp
import ml_dtypes
import numpy as np
from jax import lax
from jax.experimental import pallas as pl
from jax.experimental.pallas import tpu as pltpu
from jax.sharding import PartitionSpec as P

HALO = 2
SPAN = 2 * HALO + 1
NQ = 4
LANES = 128
F32 = jnp.float32
BF16 = jnp.bfloat16
VMEM_LIMIT = 56 * 1024 * 1024


def vmem_spec():
    return pl.BlockSpec(memory_space=pltpu.VMEM)


def smem_spec():
    return pl.BlockSpec(memory_space=pltpu.SMEM)


def params():
    return pltpu.CompilerParams(
        vmem_limit_bytes=VMEM_LIMIT, dimension_semantics=("arbitrary",)
    )


def cost(flops, nbytes, trans=0):
    return pl.CostEstimate(
        flops=int(flops), bytes_accessed=int(nbytes), transcendentals=int(trans)
    )


def tables_np(nlon, lon_count, wave_block, mmax, padded_cols):
    blocks = mmax // wave_block
    waves = np.arange(mmax).reshape(blocks, 1, wave_block)
    waves = np.broadcast_to(waves, (blocks, 2, wave_block)).reshape(-1)
    imag = np.broadcast_to(np.arange(2).reshape(1, 2, 1), (blocks, 2, wave_block)).reshape(-1)

    def table(points):
        phase = (waves[:, None].astype(np.int64) * points[None, :]) % nlon
        angle = phase * (2.0 * math.pi / nlon)
        return np.where(imag[:, None] == 0, np.cos(angle), -np.sin(angle)) / math.sqrt(nlon)

    cols = nlon // lon_count
    fwd = np.stack([table(np.arange(cols) + b * cols) for b in range(lon_count)])
    factor = np.where(waves == 0, 1.0, 2.0)[:, None]
    inv = np.stack(
        [
            (factor * table((np.arange(padded_cols) - HALO + b * cols) % nlon)).T
            for b in range(lon_count)
        ]
    )
    return fwd.astype(ml_dtypes.bfloat16), inv.astype(ml_dtypes.bfloat16)


def any_spec():
    return pl.BlockSpec(memory_space=pl.ANY)


def step_rows(rows, limit):
    return max(r for r in range(1, limit + 1) if rows % r == 0)


def first_of(array, keep):
    block = (1,) * keep + array.shape[keep:]
    return pl.BlockSpec(block, lambda t: (0,) * array.ndim)


def whole_of(array):
    return pl.BlockSpec(array.shape, lambda t: (0,) * array.ndim)


def side_by_side(parts):
    return jnp.concatenate(parts, axis=1) if len(parts) > 1 else parts[0]


def lane_blocks(cw):
    return cw % LANES == 0


def pick_kernel(index_ref, field_ref, *refs):
    refs[-1][...] = field_ref[...]


def pick(array, index, cw, begin, rows, waits):
    if not lane_blocks(cw):
        part = lax.slice_in_dim(array, begin, begin + rows, axis=0)
        return lax.dynamic_slice_in_dim(part, index * cw, cw, array.ndim - 1)
    cols = array.shape[1]
    step = step_rows(math.gcd(rows, begin), 6)
    offset = begin // step
    return pl.pallas_call(
        pick_kernel,
        grid_spec=pltpu.PrefetchScalarGridSpec(
            num_scalar_prefetch=1,
            grid=(rows // step,),
            in_specs=[pl.BlockSpec((step, cols, cw), lambda t, i: (t + offset, 0, i[0]))]
            + [any_spec()] * len(waits),
            out_specs=pl.BlockSpec((step, cols, cw), lambda t, i: (t, 0, 0)),
        ),
        out_shape=jax.ShapeDtypeStruct((rows, cols, cw), array.dtype),
        compiler_params=params(),
        cost_estimate=cost(0, 4 * rows * cols * cw),
    )(index[None], array, *waits)


def dft_kernel(lon_count, nz, waits, begin, index_ref, quad_ref, *refs):
    blocks = refs[:lon_count]
    table_ref = refs[lon_count]
    outs = refs[lon_count + 1 + waits :]
    step = pl.program_id(0)
    rows, _, cw = blocks[0].shape
    wave_rows = outs[0].shape[2]
    group = rows if cw % LANES == 0 else 1
    for first in range(0, rows, group):
        x = [side_by_side([b[first + i] for i in range(group)]) for b in blocks]
        acc = jnp.dot(table_ref[...], jnp.concatenate(x, axis=0), preferred_element_type=F32)
        for i in range(group):
            t = first + i
            scaled = acc[:, i * cw : (i + 1) * cw] * quad_ref[begin + step * rows + t]
            for d in range(nz):
                for q in range(NQ):
                    at = (d * NQ + q) * wave_rows
                    outs[d][q, t] = scaled[at : at + wave_rows].astype(BF16)


def dft(field, index, begin, received, quad, table, nz, wave_rows, cw, waits):
    rows, cols, _ = received[0].shape
    step = step_rows(math.gcd(rows, begin), 6)
    offset = begin // step
    lon_count = 1 + len(received)
    own = pl.BlockSpec((step, cols, cw), lambda t, i: (t + offset, 0, i[0]))
    if not lane_blocks(cw):
        field = pick(field, index, cw, begin, rows, [])
        own = pl.BlockSpec((step, cols, cw), lambda t, i: (t, 0, 0))
    return pl.pallas_call(
        functools.partial(dft_kernel, lon_count, nz, len(waits), begin),
        grid_spec=pltpu.PrefetchScalarGridSpec(
            num_scalar_prefetch=1,
            grid=(rows // step,),
            in_specs=[smem_spec(), own]
            + [pl.BlockSpec((step, cols, cw), lambda t, i: (t, 0, 0))] * len(received)
            + [pl.BlockSpec(table.shape, lambda t, i: (0, 0))]
            + [any_spec()] * len(waits),
            out_specs=[
                pl.BlockSpec((NQ, step, wave_rows, cw), lambda t, i: (0, t, 0, 0))
            ]
            * nz,
        ),
        out_shape=[jax.ShapeDtypeStruct((NQ, rows, wave_rows, cw), BF16)] * nz,
        compiler_params=params(),
        cost_estimate=cost(2 * table.size * rows * cw, 8 * rows * cols * cw),
    )(index[None], quad, field, *received, table, *waits)


def regroup_kernel(pieces, count, outs, *refs):
    for k, out_ref in enumerate(refs[-outs:]):
        begin = 0
        for p in range(pieces):
            for i, ref in enumerate(refs[p * count : (p + 1) * count]):
                out_ref[i, begin : begin + ref.shape[1]] = ref[k + 1]
            begin += refs[p * count].shape[1]


def regroup(pieces, waits, part=None):
    arrays = [array for piece in pieces for array in piece]
    count = len(pieces[0])
    outs, _, wave_rows, cw = arrays[0].shape
    outs -= 1
    if part is None:
        rows = sum(piece[0].shape[1] for piece in pieces)
        specs = [whole_of(a) for a in arrays]
    else:
        begin, rows = part
        block = begin // rows
        specs = [
            pl.BlockSpec((outs + 1, rows, wave_rows, cw), lambda t: (0, block, 0, 0))
        ] * len(arrays)
    shape = (count, rows, wave_rows, cw)
    return pl.pallas_call(
        functools.partial(regroup_kernel, len(pieces), count, outs),
        grid=(1,),
        in_specs=specs + [any_spec()] * len(waits),
        out_specs=[pl.BlockSpec(shape, lambda t: (0,) * len(shape))] * outs,
        out_shape=[jax.ShapeDtypeStruct(shape, BF16)] * outs,
        compiler_params=params(),
        cost_estimate=cost(0, 4 * outs * math.prod(shape)),
    )(*arrays, *waits)


def legendre_kernel(nz, pieces, waits, *refs):
    own = refs[: nz * pieces]
    refs = refs[nz * pieces :]
    others = refs[: NQ - 1]
    leg_ref, legt_ref, gr_ref, gi_ref = refs[NQ - 1 : NQ + 3]
    outs = refs[NQ + 3 + waits : -2]
    wide, result = refs[-2:]
    waves, _, lat = leg_ref.shape
    _, rows, wave_rows, cw = outs[0].shape
    span = rows * wave_rows
    for q in range(NQ):
        for d in range(nz):
            at = (q * nz + d) * span
            for piece in [others[q - 1][d]] if q else [a[0] for a in own[d::nz]]:
                length = piece.shape[0] * wave_rows
                wide[at : at + length, :] = piece.astype(F32).reshape(length, cw)
                at += length
    gain_r = gr_ref[...]
    gain_i = gi_ref[...]
    for m in range(waves):
        pair = [wide[pl.ds(r * waves + m, lat, stride=wave_rows), :] for r in range(2)]
        x = side_by_side(pair).astype(BF16)
        co = jnp.dot(leg_ref[m], x, preferred_element_type=F32)
        cr, ci = co[:, :cw], co[:, cw:]
        fr = gain_r * cr - gain_i * ci
        fi = gain_r * ci + gain_i * cr
        x = side_by_side([fr, fi]).astype(BF16)
        out = jnp.dot(legt_ref[m], x, preferred_element_type=F32)
        for r in range(2):
            result[pl.ds(r * waves + m, lat, stride=wave_rows), :] = out[:, r * cw : (r + 1) * cw]
    for q in range(NQ):
        for d in range(nz):
            at = (q * nz + d) * span
            outs[q][d] = result[at : at + span, :].reshape(rows, wave_rows, cw).astype(BF16)


def legendre_step(pieces, others, leg, legt, gr, gi, waits):
    nz = len(pieces[0])
    own = [array for piece in pieces for array in piece]
    rows, wave_rows, cw = others[0].shape[1:]
    shape = (nz, rows, wave_rows, cw)
    waves, degrees, lat = leg.shape
    return pl.pallas_call(
        functools.partial(legendre_kernel, nz, len(pieces), len(waits)),
        grid=(1,),
        in_specs=[first_of(a, 1) for a in own]
        + [whole_of(a) for a in (*others, leg, legt, gr, gi)]
        + [any_spec()] * len(waits),
        out_specs=[pl.BlockSpec(shape, lambda t: (0, 0, 0, 0))] * NQ,
        out_shape=[jax.ShapeDtypeStruct(shape, BF16)] * NQ,
        scratch_shapes=[pltpu.VMEM((lat * wave_rows, cw), F32)] * 2,
        compiler_params=params(),
        cost_estimate=cost(0, 14000000),
    )(*own, *others, leg, legt, gr, gi, *waits)


def inverse_kernel(nz, lon_count, edges_of, *refs):
    near = refs[:NQ]
    far = refs[NQ : NQ + nz - 1]
    table_ref = refs[NQ + nz - 1]
    outs = refs[NQ + nz : NQ + nz + lon_count]
    edges = refs[NQ + nz + lon_count : -1]
    wide = refs[-1]
    rows, _, cw = wide.shape
    wave_rows = near[0].shape[-2]
    cols = outs[0].shape[1]
    for t in range(rows):
        for q in range(NQ):
            for d in range(nz):
                at = (q * nz + d) * wave_rows
                block = far[d - 1][q, t] if d else near[q][0, t]
                wide[t, at : at + wave_rows, :] = block.astype(F32)
    group = rows if cw % LANES == 0 else 1
    for first in range(0, rows, group):
        x = side_by_side([wide[first + i].astype(BF16) for i in range(group)])
        acc = jnp.dot(table_ref[...], x, preferred_element_type=F32)
        for i in range(group):
            for s in range(lon_count):
                piece = acc[s * cols : (s + 1) * cols, i * cw : (i + 1) * cw]
                outs[s][first + i] = piece.astype(BF16)
    step = pl.program_id(0)
    for e, is_last in enumerate(edges_of):

        @pl.when(step == (pl.num_programs(0) - 1 if is_last else 0))
        def _(e=e, begin=rows - HALO if is_last else 0):
            for s in range(lon_count):
                edges[e * lon_count + s][...] = outs[s][begin : begin + HALO]


def inverse(near, far, table, lon_count, begin):
    nz = len(far) + 1
    _, total, wave_rows, cw = near[0].shape
    rows = far[0].shape[1]
    step = step_rows(math.gcd(rows, begin), 6)
    offset = begin // step
    cols = table.shape[0] // lon_count
    edges_of = [last for last, there in ((False, begin == 0), (True, begin + rows == total)) if there]
    specs = [pl.BlockSpec((1, step, wave_rows, cw), lambda t: (0, t + offset, 0, 0))] * NQ
    specs += [pl.BlockSpec((NQ, step, wave_rows, cw), lambda t: (0, t, 0, 0))] * (nz - 1)
    extra = lon_count * len(edges_of)
    outs = pl.pallas_call(
        functools.partial(inverse_kernel, nz, lon_count, edges_of),
        grid=(rows // step,),
        in_specs=specs + [whole_of(table)],
        out_specs=[pl.BlockSpec((step, cols, cw), lambda t: (t, 0, 0))] * lon_count
        + [pl.BlockSpec((HALO, cols, cw), lambda t: (0, 0, 0))] * extra,
        out_shape=[jax.ShapeDtypeStruct((rows, cols, cw), BF16)] * lon_count
        + [jax.ShapeDtypeStruct((HALO, cols, cw), BF16)] * extra,
        scratch_shapes=[pltpu.VMEM((step, nz * NQ * wave_rows, cw), F32)],
        compiler_params=params(),
        cost_estimate=cost(0, 14000000),
    )(*near, *far, table)
    edges = {
        last: outs[lon_count * (1 + e) : lon_count * (2 + e)] for e, last in enumerate(edges_of)
    }
    return outs[:lon_count], edges


def window_kernel(cols, place_ref, neighbour_ref, basis_ref, quad_ref, low_ref, high_ref, disco_ref, *refs):
    pieces = refs[:-2]
    out_ref, ring = refs[-2:]
    step = pl.program_id(0)
    rows = ring.shape[0] - 2 * HALO
    slots = neighbour_ref.shape[1]
    per_step = out_ref.shape[0]
    group = place_ref[0]

    @pl.when(step == 0)
    def _():
        for r in range(HALO):
            ring[r] = low_ref[r].astype(F32)
            ring[rows + HALO + r] = high_ref[r].astype(F32)
        begin = HALO
        for piece in pieces:

            def widen(r, carry, piece=piece, begin=begin):
                ring[begin + r] = piece[r].astype(F32)
                return carry

            lax.fori_loop(0, piece.shape[0], widen, 0)
            begin += piece.shape[0]

    tile = 48 if cols % 48 == 0 else 8
    for i in range(per_step):
        t = step * per_step + i
        taps = []
        for s in range(slots):
            n = neighbour_ref[t, s]
            weight = disco_ref[group, pl.ds(basis_ref[t, s], 1), :]
            taps.append((t + n // SPAN, n % SPAN, weight * quad_ref[t, s]))
        for at in range(0, cols, tile):
            acc = ring[t + HALO, pl.ds(at + HALO, tile), :]
            for row, shift, coef in taps:
                acc = acc + coef * ring[row, pl.ds(at + shift, tile), :]
            out_ref[i, pl.ds(at, tile), :] = acc.astype(BF16)


def window(place, neighbour, basis, quad, low, high, disco, pieces, cols):
    rows = sum(piece.shape[0] for piece in pieces)
    _, padded, cw = low.shape
    per_step = step_rows(rows, 2)
    return pl.pallas_call(
        functools.partial(window_kernel, cols),
        grid=(rows // per_step,),
        in_specs=[smem_spec()] * 4 + [whole_of(a) for a in (low, high, disco, *pieces)],
        out_specs=pl.BlockSpec((per_step, cols, cw), lambda t: (t, 0, 0)),
        out_shape=jax.ShapeDtypeStruct((rows, cols, cw), BF16),
        scratch_shapes=[pltpu.VMEM((rows + 2 * HALO, padded, cw), F32)],
        compiler_params=params(),
        cost_estimate=cost(0, 20000000),
    )(place, neighbour, basis, quad, low, high, disco, *pieces)


def mlp_kernel(place_ref, *refs):
    count = len(refs) - 9
    groups = refs[:count]
    gain_ref, w_in_ref, b_in_ref, w_out_ref, b_out_ref, field_ref, out_ref, spatial_ref, ordered = refs[count:]
    per_step, cols, cw = groups[0].shape
    for k in range(count):
        ordered[place_ref[k]] = groups[k][...].reshape(per_step * cols, cw)
    spatial = jnp.concatenate([ordered[k] for k in range(count)], axis=1)
    spatial_ref[...] = spatial.reshape(spatial_ref.shape)
    tokens = spatial.astype(F32)
    center = jnp.mean(tokens, axis=1, keepdims=True)
    shifted = tokens - center
    spread = jnp.mean(shifted * shifted, axis=1, keepdims=True)
    normed = (shifted * lax.rsqrt(spread + 1e-05) * gain_ref[...]).astype(BF16)
    hidden = jnp.dot(normed, w_in_ref[...], preferred_element_type=F32) + b_in_ref[...]
    hidden = jax.nn.gelu(hidden).astype(BF16)
    result = jnp.dot(hidden, w_out_ref[...], preferred_element_type=F32)
    result = result + b_out_ref[...] + field_ref[...].reshape(tokens.shape).astype(F32)
    out_ref[...] = result.astype(BF16).reshape(out_ref.shape)


def mlp(place, groups, gain, w_in, b_in, w_out, b_out, field):
    rows, cols, channels = field.shape
    cw = groups[0].shape[2]
    per_step = step_rows(rows, 2)
    block = pl.BlockSpec((per_step, cols, channels), lambda t: (t, 0, 0))
    part = pl.BlockSpec((per_step, cols, cw), lambda t: (t, 0, 0))
    return pl.pallas_call(
        mlp_kernel,
        grid=(rows // per_step,),
        in_specs=[smem_spec()]
        + [part] * len(groups)
        + [whole_of(a) for a in (gain, w_in, b_in, w_out, b_out)]
        + [block],
        out_specs=[block, block],
        out_shape=[jax.ShapeDtypeStruct(field.shape, BF16)] * 2,
        scratch_shapes=[pltpu.VMEM((len(groups), per_step * cols, cw), BF16)],
        compiler_params=params(),
        cost_estimate=cost(
            4 * field.size * w_in.shape[1], 8 * field.size, rows * cols * w_in.shape[1]
        ),
    )(place, *groups, gain, w_in, b_in, w_out, b_out, field)


def swap(array, axis, mask):
    count = lax.axis_size(axis)
    return lax.ppermute(array, axis, [(i, i ^ mask) for i in range(count)])


def shards(
    field,
    quad_weight,
    legendre,
    filter_real,
    filter_imag,
    neighbour,
    basis,
    disco_quad,
    disco_weight,
    norm_gain,
    w_in,
    b_in,
    w_out,
    b_out,
):
    rows, cols, channels = field.shape
    lon_count = lax.axis_size("lon")
    lat_count = lax.axis_size("lat")
    nz = lat_count // NQ
    wave_block, degrees, nlat = legendre.shape
    wave_rows = 2 * wave_block
    mmax = wave_block * lat_count
    nlon = cols * lon_count
    cblock = channels // lon_count
    nch = max(1, cblock // LANES)
    cw = cblock // nch
    padded_cols = (cols + 2 * HALO + 7) // 8 * 8
    lat_id = lax.axis_index("lat")
    lon_id = lax.axis_index("lon")

    fwd, inv = tables_np(nlon, lon_count, wave_block, mmax, padded_cols)
    zq = np.arange(lat_count)
    qz = (zq % nz) * NQ + zq // nz

    def permutation(masks, width):
        source = (lat_id ^ jnp.asarray(masks, jnp.int32))[:, None] * width
        source = (source + jnp.arange(width, dtype=jnp.int32)[None, :]).reshape(-1)
        return (jnp.arange(lat_count * width, dtype=jnp.int32)[None, :] == source[:, None]).astype(BF16)

    perm_fwd = permutation(zq, wave_rows)
    perm_inv = permutation(qz, wave_rows)
    perm_lat = permutation(qz, rows)

    def forward_table(table):
        parts = [
            jnp.dot(
                perm_fwd,
                lax.dynamic_index_in_dim(jnp.asarray(table), lon_id ^ s, 0, keepdims=False),
                preferred_element_type=F32,
            )
            for s in range(lon_count)
        ]
        return jnp.concatenate(parts, axis=1).astype(BF16)

    def inverse_table(table):
        parts = [
            jnp.einsum(
                "kr,ur->ku",
                lax.dynamic_index_in_dim(jnp.asarray(table), lon_id ^ s, 0, keepdims=False),
                perm_inv,
                preferred_element_type=F32,
            )
            for s in range(lon_count)
        ]
        return jnp.concatenate(parts, axis=0).astype(BF16)

    fwd = forward_table(fwd)
    inv = inverse_table(inv)
    leg = jnp.einsum("mlt,ut->mlu", legendre, perm_lat, preferred_element_type=F32).astype(BF16)
    legt = jnp.einsum("mlt,ut->mul", legendre, perm_lat, preferred_element_type=F32).astype(BF16)

    def chunk_of(array, s, j):
        start = (lon_id ^ s) * cblock + j * cw
        return lax.dynamic_slice_in_dim(array, start, cw, array.ndim - 1)

    def along(blocks):
        return [swap(block, "lat", NQ * (d + 1)) for d, block in enumerate(blocks)]

    def across(blocks):
        return [swap(block, "lat", q + 1) for q, block in enumerate(blocks)]

    disco = disco_weight.reshape(disco_weight.shape[0], lon_count * nch, cw)
    disco = jnp.transpose(disco, (1, 0, 2))
    def to_row(edge, s, shift):
        pairs = [
            (lat * lon_count + lon, (lat + shift) * lon_count + (lon ^ s))
            for lat in range(lat_count)
            for lon in range(lon_count)
            if 0 <= lat + shift < lat_count
        ]
        return lax.ppermute(edge, ("lat", "lon"), pairs)

    def channel_index(s, j):
        return ((lon_id ^ s) * nch + j).astype(jnp.int32)

    gains = [(chunk_of(filter_real, 0, j), chunk_of(filter_imag, 0, j)) for j in range(nch)]
    half = rows // 2 if rows % 2 == 0 and nch > 1 else rows
    pieces = [(begin, half) for begin in range(0, rows, half)]
    order = [(j, begin, length) for j in range(nch) for begin, length in pieces]

    def exchange(k, waits):
        j, begin, length = order[k]
        return [
            swap(pick(field, channel_index(s, j), cw, begin, length, waits), "lon", s)
            for s in range(1, lon_count)
        ]

    received = [exchange(k, [fwd] * k) for k in range(min(2, len(order)))]
    spectra = [[] for _ in range(nch)]
    waits = [leg, legt, inv] + [gain for pair in gains for gain in pair]
    for k, (j, begin, length) in enumerate(order):
        arrays = dft(
            field, channel_index(0, j), begin, received[k], quad_weight, fwd, nz, wave_rows, cw, waits
        )
        if k + 2 < len(order):
            received.append(exchange(k + 2, arrays[:1] if k else received[0]))
        waits = along(arrays[1:])
        spectra[j].append([arrays[0]] + waits)
    near = []
    gather_waits, waits = [], [arrays[0]]
    for j in range(nch):
        across_in = across(regroup(spectra[j], gather_waits))
        full = legendre_step(spectra[j], across_in, leg, legt, *gains[j], waits)
        near.append([full[0]] + across(full[1:]))
        gather_waits, waits = [full[0]], []
    groups = []
    for j in range(nch):
        waves = [[] for _ in range(lon_count)]
        edges = {}
        for begin, length in [(0, rows)]:
            far = along(regroup([near[j]], [], (begin, length)))
            parts, new_edges = inverse(near[j], far, inv, lon_count, begin)
            edges.update(new_edges)
            for s in range(lon_count):
                waves[s].append(swap(parts[s], "lon", s) if s else parts[0])
        for s in range(lon_count):
            low = to_row(edges[True][s], s, 1)
            high = to_row(edges[False][s], s, -1)
            place = channel_index(s, j)
            done = window(
                place[None], neighbour, basis, disco_quad, low, high, disco, waves[s], cols
            )
            groups.append((place, done))
    block_out, spatial = mlp(
        jnp.stack([place for place, _ in groups]),
        [done for _, done in groups],
        norm_gain[None, :],
        w_in,
        b_in[None, :],
        w_out,
        b_out[None, :],
        field,
    )
    return (block_out, spatial)


def solution(mesh):
    grid = P("lat", "lon", None)
    rows = P("lat", None)
    placed = (grid, P("lat"), P("lat", None, None), P(), P(), rows, rows, rows) + (P(),) * 6
    return jax.shard_map(
        shards,
        mesh=mesh,
        in_specs=placed,
        out_specs=(grid, grid),
        check_vma=False,
    )
```

```python
import functools
import math

import jax
import jax.numpy as jnp
import ml_dtypes
import numpy as np
from jax import lax
from jax.experimental import pallas as pl
from jax.experimental.pallas import tpu as pltpu
from jax.sharding import PartitionSpec as P

HALO = 2
SPAN = 2 * HALO + 1
NQ = 4
LANES = 128
F32 = jnp.float32
BF16 = jnp.bfloat16
VMEM_LIMIT = 56 * 1024 * 1024


def vmem_spec():
    return pl.BlockSpec(memory_space=pltpu.VMEM)


def smem_spec():
    return pl.BlockSpec(memory_space=pltpu.SMEM)


def params():
    return pltpu.CompilerParams(
        vmem_limit_bytes=VMEM_LIMIT, dimension_semantics=("arbitrary",)
    )


def cost(flops, nbytes, trans=0):
    return pl.CostEstimate(
        flops=int(flops), bytes_accessed=int(nbytes), transcendentals=int(trans)
    )


def tables_np(nlon, lon_count, wave_block, mmax, padded_cols):
    blocks = mmax // wave_block
    waves = np.arange(mmax).reshape(blocks, 1, wave_block)
    waves = np.broadcast_to(waves, (blocks, 2, wave_block)).reshape(-1)
    imag = np.broadcast_to(np.arange(2).reshape(1, 2, 1), (blocks, 2, wave_block)).reshape(-1)

    def table(points):
        phase = (waves[:, None].astype(np.int64) * points[None, :]) % nlon
        angle = phase * (2.0 * math.pi / nlon)
        return np.where(imag[:, None] == 0, np.cos(angle), -np.sin(angle)) / math.sqrt(nlon)

    cols = nlon // lon_count
    fwd = np.stack([table(np.arange(cols) + b * cols) for b in range(lon_count)])
    factor = np.where(waves == 0, 1.0, 2.0)[:, None]
    inv = np.stack(
        [
            (factor * table((np.arange(padded_cols) - HALO + b * cols) % nlon)).T
            for b in range(lon_count)
        ]
    )
    return fwd.astype(ml_dtypes.bfloat16), inv.astype(ml_dtypes.bfloat16)


def any_spec():
    return pl.BlockSpec(memory_space=pl.ANY)


def step_rows(rows, limit):
    return max(r for r in range(1, limit + 1) if rows % r == 0)


def first_of(array, keep):
    block = (1,) * keep + array.shape[keep:]
    return pl.BlockSpec(block, lambda t: (0,) * array.ndim)


def whole_of(array):
    return pl.BlockSpec(array.shape, lambda t: (0,) * array.ndim)


def side_by_side(parts):
    return jnp.concatenate(parts, axis=1) if len(parts) > 1 else parts[0]


def lane_blocks(cw):
    return cw % LANES == 0


def pick_kernel(index_ref, field_ref, *refs):
    refs[-1][...] = field_ref[...]


def pick(array, index, cw, waits):
    if not lane_blocks(cw):
        return lax.dynamic_slice_in_dim(array, index * cw, cw, array.ndim - 1)
    rows, cols, _ = array.shape
    step = step_rows(rows, 6)
    return pl.pallas_call(
        pick_kernel,
        grid_spec=pltpu.PrefetchScalarGridSpec(
            num_scalar_prefetch=1,
            grid=(rows // step,),
            in_specs=[pl.BlockSpec((step, cols, cw), lambda t, i: (t, 0, i[0]))]
            + [any_spec()] * len(waits),
            out_specs=pl.BlockSpec((step, cols, cw), lambda t, i: (t, 0, 0)),
        ),
        out_shape=jax.ShapeDtypeStruct((rows, cols, cw), array.dtype),
        compiler_params=params(),
        cost_estimate=cost(0, 4 * rows * cols * cw),
    )(index[None], array, *waits)


def rows_kernel(first_in, last_in, *refs):
    first_ref, last_ref = refs[-2:]
    first_ref[...] = first_in[...]
    last_ref[...] = last_in[...]


def edge_rows(wave, waits):
    rows, cols, cw = wave.shape
    edge = jax.ShapeDtypeStruct((HALO, cols, cw), wave.dtype)
    last = rows // HALO - 1
    block = (HALO, cols, cw)
    return pl.pallas_call(
        rows_kernel,
        grid=(1,),
        in_specs=[
            pl.BlockSpec(block, lambda t: (0, 0, 0)),
            pl.BlockSpec(block, lambda t: (last, 0, 0)),
        ]
        + [any_spec()] * len(waits),
        out_specs=[pl.BlockSpec(block, lambda t: (0, 0, 0))] * 2,
        out_shape=[edge, edge],
        compiler_params=params(),
        cost_estimate=cost(0, 8 * edge.size),
    )(wave, wave, *waits)


def dft_kernel(lon_count, nz, waits, index_ref, quad_ref, *refs):
    blocks = refs[:lon_count]
    table_ref = refs[lon_count]
    outs = refs[lon_count + 1 + waits :]
    step = pl.program_id(0)
    rows, _, cw = blocks[0].shape
    wave_rows = outs[0].shape[2]
    group = rows if cw % LANES == 0 else 1
    for first in range(0, rows, group):
        x = [side_by_side([b[first + i] for i in range(group)]) for b in blocks]
        acc = jnp.dot(table_ref[...], jnp.concatenate(x, axis=0), preferred_element_type=F32)
        for i in range(group):
            t = first + i
            scaled = acc[:, i * cw : (i + 1) * cw] * quad_ref[step * rows + t]
            for d in range(nz):
                for q in range(NQ):
                    at = (d * NQ + q) * wave_rows
                    outs[d][q, t] = scaled[at : at + wave_rows].astype(BF16)


def dft(field, index, received, quad, table, nz, wave_rows, cw, waits):
    rows, cols, _ = field.shape
    step = step_rows(rows, 6)
    lon_count = 1 + len(received)
    own = pl.BlockSpec((step, cols, cw), lambda t, i: (t, 0, i[0]))
    if not lane_blocks(cw):
        field = pick(field, index, cw, [])
        own = pl.BlockSpec((step, cols, cw), lambda t, i: (t, 0, 0))
    return pl.pallas_call(
        functools.partial(dft_kernel, lon_count, nz, len(waits)),
        grid_spec=pltpu.PrefetchScalarGridSpec(
            num_scalar_prefetch=1,
            grid=(rows // step,),
            in_specs=[smem_spec(), own]
            + [pl.BlockSpec((step, cols, cw), lambda t, i: (t, 0, 0))] * len(received)
            + [pl.BlockSpec(table.shape, lambda t, i: (0, 0))]
            + [any_spec()] * len(waits),
            out_specs=[
                pl.BlockSpec((NQ, step, wave_rows, cw), lambda t, i: (0, t, 0, 0))
            ]
            * nz,
        ),
        out_shape=[jax.ShapeDtypeStruct((NQ, rows, wave_rows, cw), BF16)] * nz,
        compiler_params=params(),
        cost_estimate=cost(2 * table.size * rows * cw, 8 * rows * cols * cw),
    )(index[None], quad, field, *received, table, *waits)


def regroup_kernel(count, outs, *refs):
    sources = refs[:count]
    for k, out_ref in enumerate(refs[-outs:]):
        for i, ref in enumerate(sources):
            out_ref[i] = ref[k + 1]


def regroup(arrays, waits):
    count = len(arrays)
    outs = arrays[0].shape[0] - 1
    shape = (count,) + arrays[0].shape[1:]
    return pl.pallas_call(
        functools.partial(regroup_kernel, count, outs),
        grid=(1,),
        in_specs=[whole_of(a) for a in arrays] + [any_spec()] * len(waits),
        out_specs=[pl.BlockSpec(shape, lambda t: (0,) * len(shape))] * outs,
        out_shape=[jax.ShapeDtypeStruct(shape, BF16)] * outs,
        compiler_params=params(),
        cost_estimate=cost(0, 4 * outs * math.prod(shape)),
    )(*arrays, *waits)


def legendre_kernel(nz, waits, *refs):
    own = refs[:nz]
    others = refs[nz : nz + NQ - 1]
    leg_ref, legt_ref, gr_ref, gi_ref = refs[nz + NQ - 1 : nz + NQ + 3]
    outs = refs[nz + NQ + 3 + waits : -2]
    wide, result = refs[-2:]
    waves, _, lat = leg_ref.shape
    _, rows, wave_rows, cw = outs[0].shape
    span = rows * wave_rows
    for q in range(NQ):
        for d in range(nz):
            at = (q * nz + d) * span
            piece = others[q - 1][d] if q else own[d][0]
            wide[at : at + span, :] = piece.astype(F32).reshape(span, cw)
    gain_r = gr_ref[...]
    gain_i = gi_ref[...]
    for m in range(waves):
        pair = [wide[pl.ds(r * waves + m, lat, stride=wave_rows), :] for r in range(2)]
        x = side_by_side(pair).astype(BF16)
        co = jnp.dot(leg_ref[m], x, preferred_element_type=F32)
        cr, ci = co[:, :cw], co[:, cw:]
        fr = gain_r * cr - gain_i * ci
        fi = gain_r * ci + gain_i * cr
        x = side_by_side([fr, fi]).astype(BF16)
        out = jnp.dot(legt_ref[m], x, preferred_element_type=F32)
        for r in range(2):
            result[pl.ds(r * waves + m, lat, stride=wave_rows), :] = out[:, r * cw : (r + 1) * cw]
    for q in range(NQ):
        for d in range(nz):
            at = (q * nz + d) * span
            outs[q][d] = result[at : at + span, :].reshape(rows, wave_rows, cw).astype(BF16)


def legendre_step(own, others, leg, legt, gr, gi, waits):
    nz = len(own)
    _, rows, wave_rows, cw = own[0].shape
    shape = (nz, rows, wave_rows, cw)
    waves, degrees, lat = leg.shape
    return pl.pallas_call(
        functools.partial(legendre_kernel, nz, len(waits)),
        grid=(1,),
        in_specs=[first_of(a, 1) for a in own]
        + [whole_of(a) for a in (*others, leg, legt, gr, gi)]
        + [any_spec()] * len(waits),
        out_specs=[pl.BlockSpec(shape, lambda t: (0, 0, 0, 0))] * NQ,
        out_shape=[jax.ShapeDtypeStruct(shape, BF16)] * NQ,
        scratch_shapes=[pltpu.VMEM((lat * wave_rows, cw), F32)] * 2,
        compiler_params=params(),
        cost_estimate=cost(0, 14000000),
    )(*own, *others, leg, legt, gr, gi, *waits)


def inverse_kernel(nz, lon_count, waits, *refs):
    near = refs[:NQ]
    far = refs[NQ : NQ + nz - 1]
    table_ref = refs[NQ + nz - 1]
    outs = refs[NQ + nz + waits : NQ + nz + waits + lon_count]
    first_ref, last_ref, wide = refs[-3:]
    rows, _, cw = wide.shape
    wave_rows = near[0].shape[-2]
    cols = outs[0].shape[1]
    for t in range(rows):
        for q in range(NQ):
            for d in range(nz):
                at = (q * nz + d) * wave_rows
                block = far[d - 1][q, t] if d else near[q][0, t]
                wide[t, at : at + wave_rows, :] = block.astype(F32)
    group = rows if cw % LANES == 0 else 1
    for first in range(0, rows, group):
        x = side_by_side([wide[first + i].astype(BF16) for i in range(group)])
        acc = jnp.dot(table_ref[...], x, preferred_element_type=F32)
        for i in range(group):
            for s in range(lon_count):
                piece = acc[s * cols : (s + 1) * cols, i * cw : (i + 1) * cw]
                outs[s][first + i] = piece.astype(BF16)
    step = pl.program_id(0)

    @pl.when(step == 0)
    def _():
        first_ref[...] = outs[0][:HALO]

    @pl.when(step == pl.num_programs(0) - 1)
    def _():
        last_ref[...] = outs[0][rows - HALO :]


def inverse(near, far, table, lon_count, waits):
    nz = len(far) + 1
    _, rows, wave_rows, cw = near[0].shape
    step = step_rows(rows, 6)
    cols = table.shape[0] // lon_count
    specs = [pl.BlockSpec((1, step, wave_rows, cw), lambda t: (0, t, 0, 0))] * NQ
    specs += [pl.BlockSpec((NQ, step, wave_rows, cw), lambda t: (0, t, 0, 0))] * (nz - 1)
    return pl.pallas_call(
        functools.partial(inverse_kernel, nz, lon_count, len(waits)),
        grid=(rows // step,),
        in_specs=specs + [whole_of(table)] + [any_spec()] * len(waits),
        out_specs=[pl.BlockSpec((step, cols, cw), lambda t: (t, 0, 0))] * lon_count
        + [pl.BlockSpec((HALO, cols, cw), lambda t: (0, 0, 0))] * 2,
        out_shape=[jax.ShapeDtypeStruct((rows, cols, cw), BF16)] * lon_count
        + [jax.ShapeDtypeStruct((HALO, cols, cw), BF16)] * 2,
        scratch_shapes=[pltpu.VMEM((step, nz * NQ * wave_rows, cw), F32)],
        compiler_params=params(),
        cost_estimate=cost(0, 14000000),
    )(*near, *far, table, *waits)


def window_kernel(cols, place_ref, neighbour_ref, basis_ref, quad_ref, wave_ref, low_ref, high_ref, disco_ref, out_ref, ring):
    step = pl.program_id(0)
    rows = wave_ref.shape[0]
    slots = neighbour_ref.shape[1]
    per_step = out_ref.shape[0]
    group = place_ref[0]

    @pl.when(step == 0)
    def _():
        for r in range(HALO):
            ring[r] = low_ref[r].astype(F32)
            ring[HALO + r] = wave_ref[r].astype(F32)
            ring[rows + HALO + r] = high_ref[r].astype(F32)

    for i in range(per_step):
        t = step * per_step + i

        @pl.when(t + HALO < rows)
        def _(t=t):
            ring[t + 2 * HALO] = wave_ref[t + HALO].astype(F32)

    tile = 48 if cols % 48 == 0 else 8
    for i in range(per_step):
        t = step * per_step + i
        taps = []
        for s in range(slots):
            n = neighbour_ref[t, s]
            weight = disco_ref[group, pl.ds(basis_ref[t, s], 1), :]
            taps.append((t + n // SPAN, n % SPAN, weight * quad_ref[t, s]))
        for at in range(0, cols, tile):
            acc = ring[t + HALO, pl.ds(at + HALO, tile), :]
            for row, shift, coef in taps:
                acc = acc + coef * ring[row, pl.ds(at + shift, tile), :]
            out_ref[i, pl.ds(at, tile), :] = acc.astype(BF16)


def window(place, neighbour, basis, quad, wave, low, high, disco, cols):
    rows, padded, cw = wave.shape
    per_step = step_rows(rows, 2)
    return pl.pallas_call(
        functools.partial(window_kernel, cols),
        grid=(rows // per_step,),
        in_specs=[smem_spec()] * 4 + [whole_of(a) for a in (wave, low, high, disco)],
        out_specs=pl.BlockSpec((per_step, cols, cw), lambda t: (t, 0, 0)),
        out_shape=jax.ShapeDtypeStruct((rows, cols, cw), BF16),
        scratch_shapes=[pltpu.VMEM((rows + 2 * HALO, padded, cw), F32)],
        compiler_params=params(),
        cost_estimate=cost(0, 20000000),
    )(place, neighbour, basis, quad, wave, low, high, disco)


def mlp_kernel(place_ref, *refs):
    count = len(refs) - 9
    groups = refs[:count]
    gain_ref, w_in_ref, b_in_ref, w_out_ref, b_out_ref, field_ref, out_ref, spatial_ref, ordered = refs[count:]
    per_step, cols, cw = groups[0].shape
    for k in range(count):
        ordered[place_ref[k]] = groups[k][...].reshape(per_step * cols, cw)
    spatial = jnp.concatenate([ordered[k] for k in range(count)], axis=1)
    spatial_ref[...] = spatial.reshape(spatial_ref.shape)
    tokens = spatial.astype(F32)
    center = jnp.mean(tokens, axis=1, keepdims=True)
    shifted = tokens - center
    spread = jnp.mean(shifted * shifted, axis=1, keepdims=True)
    normed = (shifted * lax.rsqrt(spread + 1e-05) * gain_ref[...]).astype(BF16)
    hidden = jnp.dot(normed, w_in_ref[...], preferred_element_type=F32) + b_in_ref[...]
    hidden = jax.nn.gelu(hidden).astype(BF16)
    result = jnp.dot(hidden, w_out_ref[...], preferred_element_type=F32)
    result = result + b_out_ref[...] + field_ref[...].reshape(tokens.shape).astype(F32)
    out_ref[...] = result.astype(BF16).reshape(out_ref.shape)


def mlp(place, groups, gain, w_in, b_in, w_out, b_out, field):
    rows, cols, channels = field.shape
    cw = groups[0].shape[2]
    per_step = step_rows(rows, 2)
    block = pl.BlockSpec((per_step, cols, channels), lambda t: (t, 0, 0))
    part = pl.BlockSpec((per_step, cols, cw), lambda t: (t, 0, 0))
    return pl.pallas_call(
        mlp_kernel,
        grid=(rows // per_step,),
        in_specs=[smem_spec()]
        + [part] * len(groups)
        + [whole_of(a) for a in (gain, w_in, b_in, w_out, b_out)]
        + [block],
        out_specs=[block, block],
        out_shape=[jax.ShapeDtypeStruct(field.shape, BF16)] * 2,
        scratch_shapes=[pltpu.VMEM((len(groups), per_step * cols, cw), BF16)],
        compiler_params=params(),
        cost_estimate=cost(
            4 * field.size * w_in.shape[1], 8 * field.size, rows * cols * w_in.shape[1]
        ),
    )(place, *groups, gain, w_in, b_in, w_out, b_out, field)


def swap(array, axis, mask):
    count = lax.axis_size(axis)
    return lax.ppermute(array, axis, [(i, i ^ mask) for i in range(count)])


def shards(
    field,
    quad_weight,
    legendre,
    filter_real,
    filter_imag,
    neighbour,
    basis,
    disco_quad,
    disco_weight,
    norm_gain,
    w_in,
    b_in,
    w_out,
    b_out,
):
    rows, cols, channels = field.shape
    lon_count = lax.axis_size("lon")
    lat_count = lax.axis_size("lat")
    nz = lat_count // NQ
    wave_block, degrees, nlat = legendre.shape
    wave_rows = 2 * wave_block
    mmax = wave_block * lat_count
    nlon = cols * lon_count
    cblock = channels // lon_count
    nch = max(1, cblock // LANES)
    cw = cblock // nch
    padded_cols = (cols + 2 * HALO + 7) // 8 * 8
    lat_id = lax.axis_index("lat")
    lon_id = lax.axis_index("lon")

    fwd, inv = tables_np(nlon, lon_count, wave_block, mmax, padded_cols)
    zq = np.arange(lat_count)
    qz = (zq % nz) * NQ + zq // nz

    def permutation(masks, width):
        source = (lat_id ^ jnp.asarray(masks, jnp.int32))[:, None] * width
        source = (source + jnp.arange(width, dtype=jnp.int32)[None, :]).reshape(-1)
        return (jnp.arange(lat_count * width, dtype=jnp.int32)[None, :] == source[:, None]).astype(BF16)

    perm_fwd = permutation(zq, wave_rows)
    perm_inv = permutation(qz, wave_rows)
    perm_lat = permutation(qz, rows)

    def forward_table(table):
        parts = [
            jnp.dot(
                perm_fwd,
                lax.dynamic_index_in_dim(jnp.asarray(table), lon_id ^ s, 0, keepdims=False),
                preferred_element_type=F32,
            )
            for s in range(lon_count)
        ]
        return jnp.concatenate(parts, axis=1).astype(BF16)

    def inverse_table(table):
        parts = [
            jnp.einsum(
                "kr,ur->ku",
                lax.dynamic_index_in_dim(jnp.asarray(table), lon_id ^ s, 0, keepdims=False),
                perm_inv,
                preferred_element_type=F32,
            )
            for s in range(lon_count)
        ]
        return jnp.concatenate(parts, axis=0).astype(BF16)

    fwd = forward_table(fwd)
    inv = inverse_table(inv)
    leg = jnp.einsum("mlt,ut->mlu", legendre, perm_lat, preferred_element_type=F32).astype(BF16)
    legt = jnp.einsum("mlt,ut->mul", legendre, perm_lat, preferred_element_type=F32).astype(BF16)

    def chunk_of(array, s, j):
        start = (lon_id ^ s) * cblock + j * cw
        return lax.dynamic_slice_in_dim(array, start, cw, array.ndim - 1)

    def along(blocks):
        return [swap(block, "lat", NQ * (d + 1)) for d, block in enumerate(blocks)]

    def across(blocks):
        return [swap(block, "lat", q + 1) for q, block in enumerate(blocks)]

    disco = disco_weight.reshape(disco_weight.shape[0], lon_count * nch, cw)
    disco = jnp.transpose(disco, (1, 0, 2))
    up = [(i, i + 1) for i in range(lat_count - 1)]
    down = [(i + 1, i) for i in range(lat_count - 1)]

    def convolved(wave, edges, s, j):
        first, last = edges
        low = lax.ppermute(last, "lat", up)
        high = lax.ppermute(first, "lat", down)
        place = channel_index(s, j)
        done = window(
            place[None], neighbour, basis, disco_quad, wave, low, high, disco, cols
        )
        return place, done

    def channel_index(s, j):
        return ((lon_id ^ s) * nch + j).astype(jnp.int32)

    received, waits = [], []
    for j in range(nch):
        received.append(
            [
                swap(pick(field, channel_index(s, j), cw, waits), "lon", s)
                for s in range(1, lon_count)
            ]
        )
        waits = [fwd]
    gains = [(chunk_of(filter_real, 0, j), chunk_of(filter_imag, 0, j)) for j in range(nch)]
    spectra = []
    waits = [leg, legt, inv] + [gain for pair in gains for gain in pair]
    for j in range(nch):
        arrays = dft(
            field, channel_index(0, j), received[j], quad_weight, fwd, nz, wave_rows, cw, waits
        )
        spectra.append([arrays[0]] + along(arrays[1:]))
        waits = [spectra[-1][1]]
        latest = arrays[0]
    near = []
    waits = [latest]
    for j in range(nch):
        full = legendre_step(
            spectra[j], across(regroup(spectra[j], waits)), leg, legt, *gains[j], []
        )
        near.append([full[0]] + across(full[1:]))
        waits = []
    groups, sent, waits = [], [], []
    for j in range(nch):
        *parts, first, last = inverse(
            near[j], along(regroup(near[j], [])), inv, lon_count, waits
        )
        sent.append([swap(parts[s], "lon", s) for s in range(1, lon_count)])
        groups.append(convolved(parts[0], (first, last), 0, j))
        waits = [groups[-1][1]]
    for j in range(nch):
        waits = [done for _, done in groups] if j == nch - 1 else []
        for s, wave in enumerate(sent[j], 1):
            groups.append(convolved(wave, edge_rows(wave, waits), s, j))
    block_out, spatial = mlp(
        jnp.stack([place for place, _ in groups]),
        [done for _, done in groups],
        norm_gain[None, :],
        w_in,
        b_in[None, :],
        w_out,
        b_out[None, :],
        field,
    )
    return (block_out, spatial)


def solution(mesh):
    grid = P("lat", "lon", None)
    rows = P("lat", None)
    placed = (grid, P("lat"), P("lat", None, None), P(), P(), rows, rows, rows) + (P(),) * 6
    return jax.shard_map(
        shards,
        mesh=mesh,
        in_specs=placed,
        out_specs=(grid, grid),
        check_vma=False,
    )
```

```python
import functools
import math

import jax
import jax.numpy as jnp
import ml_dtypes
import numpy as np
from jax import lax
from jax.experimental import pallas as pl
from jax.experimental.pallas import tpu as pltpu
from jax.sharding import PartitionSpec as P

HALO = 2
SPAN = 2 * HALO + 1
NQ = 4
LANES = 128
F32 = jnp.float32
BF16 = jnp.bfloat16
VMEM_LIMIT = 56 * 1024 * 1024


def vmem_spec():
    return pl.BlockSpec(memory_space=pltpu.VMEM)


def smem_spec():
    return pl.BlockSpec(memory_space=pltpu.SMEM)


def params():
    return pltpu.CompilerParams(
        vmem_limit_bytes=VMEM_LIMIT, dimension_semantics=("arbitrary",)
    )


def cost(flops, nbytes, trans=0):
    return pl.CostEstimate(
        flops=int(flops), bytes_accessed=int(nbytes), transcendentals=int(trans)
    )


def tables_np(nlon, lon_count, wave_block, mmax, padded_cols):
    blocks = mmax // wave_block
    waves = np.arange(mmax).reshape(blocks, 1, wave_block)
    waves = np.broadcast_to(waves, (blocks, 2, wave_block)).reshape(-1)
    imag = np.broadcast_to(np.arange(2).reshape(1, 2, 1), (blocks, 2, wave_block)).reshape(-1)

    def table(points):
        phase = (waves[:, None].astype(np.int64) * points[None, :]) % nlon
        angle = phase * (2.0 * math.pi / nlon)
        return np.where(imag[:, None] == 0, np.cos(angle), -np.sin(angle)) / math.sqrt(nlon)

    cols = nlon // lon_count
    fwd = np.stack([table(np.arange(cols) + b * cols) for b in range(lon_count)])
    factor = np.where(waves == 0, 1.0, 2.0)[:, None]
    inv = np.stack(
        [
            (factor * table((np.arange(padded_cols) - HALO + b * cols) % nlon)).T
            for b in range(lon_count)
        ]
    )
    return fwd.astype(ml_dtypes.bfloat16), inv.astype(ml_dtypes.bfloat16)


def any_spec():
    return pl.BlockSpec(memory_space=pl.ANY)


def step_rows(rows, limit):
    return max(r for r in range(1, limit + 1) if rows % r == 0)


def first_of(array, keep):
    block = (1,) * keep + array.shape[keep:]
    return pl.BlockSpec(block, lambda t: (0,) * array.ndim)


def whole_of(array):
    return pl.BlockSpec(array.shape, lambda t: (0,) * array.ndim)


def side_by_side(parts):
    return jnp.concatenate(parts, axis=1) if len(parts) > 1 else parts[0]


def lane_blocks(cw):
    return cw % LANES == 0


def pick_kernel(index_ref, field_ref, *refs):
    refs[-1][...] = field_ref[...]


def pick(array, index, cw, waits):
    if not lane_blocks(cw):
        return lax.dynamic_slice_in_dim(array, index * cw, cw, array.ndim - 1)
    rows, cols, _ = array.shape
    step = step_rows(rows, 6)
    return pl.pallas_call(
        pick_kernel,
        grid_spec=pltpu.PrefetchScalarGridSpec(
            num_scalar_prefetch=1,
            grid=(rows // step,),
            in_specs=[pl.BlockSpec((step, cols, cw), lambda t, i: (t, 0, i[0]))]
            + [any_spec()] * len(waits),
            out_specs=pl.BlockSpec((step, cols, cw), lambda t, i: (t, 0, 0)),
        ),
        out_shape=jax.ShapeDtypeStruct((rows, cols, cw), array.dtype),
        compiler_params=params(),
        cost_estimate=cost(0, 4 * rows * cols * cw),
    )(index[None], array, *waits)


def dft_kernel(lon_count, nz, waits, index_ref, quad_ref, *refs):
    blocks = refs[:lon_count]
    table_ref = refs[lon_count]
    outs = refs[lon_count + 1 + waits :]
    step = pl.program_id(0)
    rows, _, cw = blocks[0].shape
    wave_rows = outs[0].shape[2]
    group = rows if cw % LANES == 0 else 1
    for first in range(0, rows, group):
        x = [side_by_side([b[first + i] for i in range(group)]) for b in blocks]
        acc = jnp.dot(table_ref[...], jnp.concatenate(x, axis=0), preferred_element_type=F32)
        for i in range(group):
            t = first + i
            scaled = acc[:, i * cw : (i + 1) * cw] * quad_ref[step * rows + t]
            for d in range(nz):
                for q in range(NQ):
                    at = (d * NQ + q) * wave_rows
                    outs[d][q, t] = scaled[at : at + wave_rows].astype(BF16)


def dft(field, index, received, quad, table, nz, wave_rows, cw, waits):
    rows, cols, _ = field.shape
    step = step_rows(rows, 6)
    lon_count = 1 + len(received)
    own = pl.BlockSpec((step, cols, cw), lambda t, i: (t, 0, i[0]))
    if not lane_blocks(cw):
        field = pick(field, index, cw, [])
        own = pl.BlockSpec((step, cols, cw), lambda t, i: (t, 0, 0))
    return pl.pallas_call(
        functools.partial(dft_kernel, lon_count, nz, len(waits)),
        grid_spec=pltpu.PrefetchScalarGridSpec(
            num_scalar_prefetch=1,
            grid=(rows // step,),
            in_specs=[smem_spec(), own]
            + [pl.BlockSpec((step, cols, cw), lambda t, i: (t, 0, 0))] * len(received)
            + [pl.BlockSpec(table.shape, lambda t, i: (0, 0))]
            + [any_spec()] * len(waits),
            out_specs=[
                pl.BlockSpec((NQ, step, wave_rows, cw), lambda t, i: (0, t, 0, 0))
            ]
            * nz,
        ),
        out_shape=[jax.ShapeDtypeStruct((NQ, rows, wave_rows, cw), BF16)] * nz,
        compiler_params=params(),
        cost_estimate=cost(2 * table.size * rows * cw, 8 * rows * cols * cw),
    )(index[None], quad, field, *received, table, *waits)


def regroup_kernel(count, outs, *refs):
    sources = refs[:count]
    for k, out_ref in enumerate(refs[-outs:]):
        for i, ref in enumerate(sources):
            out_ref[i] = ref[k + 1]


def regroup(arrays, waits):
    count = len(arrays)
    outs = arrays[0].shape[0] - 1
    shape = (count,) + arrays[0].shape[1:]
    return pl.pallas_call(
        functools.partial(regroup_kernel, count, outs),
        grid=(1,),
        in_specs=[whole_of(a) for a in arrays] + [any_spec()] * len(waits),
        out_specs=[pl.BlockSpec(shape, lambda t: (0,) * len(shape))] * outs,
        out_shape=[jax.ShapeDtypeStruct(shape, BF16)] * outs,
        compiler_params=params(),
        cost_estimate=cost(0, 4 * outs * math.prod(shape)),
    )(*arrays, *waits)


def legendre_kernel(nz, waits, *refs):
    own = refs[:nz]
    others = refs[nz : nz + NQ - 1]
    leg_ref, legt_ref, gr_ref, gi_ref = refs[nz + NQ - 1 : nz + NQ + 3]
    outs = refs[nz + NQ + 3 + waits : -2]
    wide, result = refs[-2:]
    waves, _, lat = leg_ref.shape
    _, rows, wave_rows, cw = outs[0].shape
    span = rows * wave_rows
    for q in range(NQ):
        for d in range(nz):
            at = (q * nz + d) * span
            piece = others[q - 1][d] if q else own[d][0]
            wide[at : at + span, :] = piece.astype(F32).reshape(span, cw)
    gain_r = gr_ref[...]
    gain_i = gi_ref[...]
    for m in range(waves):
        pair = [wide[pl.ds(r * waves + m, lat, stride=wave_rows), :] for r in range(2)]
        x = side_by_side(pair).astype(BF16)
        co = jnp.dot(leg_ref[m], x, preferred_element_type=F32)
        cr, ci = co[:, :cw], co[:, cw:]
        fr = gain_r * cr - gain_i * ci
        fi = gain_r * ci + gain_i * cr
        x = side_by_side([fr, fi]).astype(BF16)
        out = jnp.dot(legt_ref[m], x, preferred_element_type=F32)
        for r in range(2):
            result[pl.ds(r * waves + m, lat, stride=wave_rows), :] = out[:, r * cw : (r + 1) * cw]
    for q in range(NQ):
        for d in range(nz):
            at = (q * nz + d) * span
            outs[q][d] = result[at : at + span, :].reshape(rows, wave_rows, cw).astype(BF16)


def legendre_step(own, others, leg, legt, gr, gi, waits):
    nz = len(own)
    _, rows, wave_rows, cw = own[0].shape
    shape = (nz, rows, wave_rows, cw)
    waves, degrees, lat = leg.shape
    return pl.pallas_call(
        functools.partial(legendre_kernel, nz, len(waits)),
        grid=(1,),
        in_specs=[first_of(a, 1) for a in own]
        + [whole_of(a) for a in (*others, leg, legt, gr, gi)]
        + [any_spec()] * len(waits),
        out_specs=[pl.BlockSpec(shape, lambda t: (0, 0, 0, 0))] * NQ,
        out_shape=[jax.ShapeDtypeStruct(shape, BF16)] * NQ,
        scratch_shapes=[pltpu.VMEM((lat * wave_rows, cw), F32)] * 2,
        compiler_params=params(),
        cost_estimate=cost(0, 14000000),
    )(*own, *others, leg, legt, gr, gi, *waits)


def inverse_kernel(nz, lon_count, split, waits, *refs):
    near = refs[:NQ]
    far = refs[NQ : NQ + nz - 1]
    table_ref = refs[NQ + nz - 1]
    own_ref, first_ref, last_ref, *apart, wide = refs[NQ + nz + waits :]
    step = pl.program_id(0)
    rows, _, cw = wide.shape
    wave_rows = near[0].shape[-2]
    cols = own_ref.shape[1]
    total = rows * pl.num_programs(0)
    for t in range(rows):
        for q in range(NQ):
            for d in range(nz):
                at = (q * nz + d) * wave_rows
                block = far[d - 1][q, t] if d else near[q][0, t]
                wide[t, at : at + wave_rows, :] = block.astype(F32)
    def put(s, i, value):
        if s == 0:
            own_ref[i] = value
            return
        if not split:
            apart[s - 1][i] = value
            return
        edge_ref, inner_ref = apart[2 * s - 2 : 2 * s]
        r = step * rows + i

        @pl.when(r < HALO)
        def _():
            edge_ref[r] = value

        @pl.when(r >= total - HALO)
        def _():
            edge_ref[r - total + 2 * HALO] = value

        @pl.when((r >= HALO) & (r < total - HALO))
        def _():
            inner_ref[r - HALO] = value

    group = rows if cw % LANES == 0 else 1
    for first in range(0, rows, group):
        x = side_by_side([wide[first + i].astype(BF16) for i in range(group)])
        acc = jnp.dot(table_ref[...], x, preferred_element_type=F32)
        for i in range(group):
            for s in range(lon_count):
                piece = acc[s * cols : (s + 1) * cols, i * cw : (i + 1) * cw]
                put(s, first + i, piece.astype(BF16))
    step = pl.program_id(0)

    @pl.when(step == 0)
    def _():
        first_ref[...] = own_ref[:HALO]

    @pl.when(step == pl.num_programs(0) - 1)
    def _():
        last_ref[...] = own_ref[rows - HALO :]


def inverse(near, far, table, lon_count, split, waits):
    nz = len(far) + 1
    _, rows, wave_rows, cw = near[0].shape
    step = step_rows(rows, 6)
    cols = table.shape[0] // lon_count
    extra = [HALO, HALO] + ([2 * HALO, rows - 2 * HALO] if split else [rows]) * (lon_count - 1)
    extra = [jax.ShapeDtypeStruct((r, cols, cw), BF16) for r in extra]
    moving = pl.BlockSpec((step, cols, cw), lambda t: (t, 0, 0))
    specs = [pl.BlockSpec((1, step, wave_rows, cw), lambda t: (0, t, 0, 0))] * NQ
    specs += [pl.BlockSpec((NQ, step, wave_rows, cw), lambda t: (0, t, 0, 0))] * (nz - 1)
    return pl.pallas_call(
        functools.partial(inverse_kernel, nz, lon_count, split, len(waits)),
        grid=(rows // step,),
        in_specs=specs + [whole_of(table)] + [any_spec()] * len(waits),
        out_specs=[moving]
        + [
            moving if a.shape[0] == rows else pl.BlockSpec(a.shape, lambda t: (0, 0, 0))
            for a in extra
        ],
        out_shape=[jax.ShapeDtypeStruct((rows, cols, cw), BF16)] + extra,
        scratch_shapes=[pltpu.VMEM((step, nz * NQ * wave_rows, cw), F32)],
        compiler_params=params(),
        cost_estimate=cost(0, 14000000),
    )(*near, *far, table, *waits)


def window_kernel(cols, arrays, place_ref, neighbour_ref, basis_ref, quad_ref, low_ref, high_ref, disco_ref, *refs):
    wave_ref = refs[arrays - 1]
    edge_ref = refs[0]
    out_ref, ring = refs[-2:]
    step = pl.program_id(0)
    rows = ring.shape[0] - 2 * HALO
    inner = wave_ref.shape[0]
    skipped = (rows - inner) // 2
    slots = neighbour_ref.shape[1]
    per_step = out_ref.shape[0]
    group = place_ref[0]

    @pl.when(step == 0)
    def _():
        for r in range(HALO):
            ring[r] = low_ref[r].astype(F32)
            ring[HALO + r] = edge_ref[r].astype(F32)
            ring[rows + HALO + r] = high_ref[r].astype(F32)
            if skipped:
                ring[rows + r] = edge_ref[HALO + r].astype(F32)

    for i in range(per_step):
        t = step * per_step + i

        @pl.when(t + HALO < rows - skipped)
        def _(t=t):
            ring[t + 2 * HALO] = wave_ref[t + HALO - skipped].astype(F32)

    tile = 48 if cols % 48 == 0 else 8
    for i in range(per_step):
        t = step * per_step + i
        taps = []
        for s in range(slots):
            n = neighbour_ref[t, s]
            weight = disco_ref[group, pl.ds(basis_ref[t, s], 1), :]
            taps.append((t + n // SPAN, n % SPAN, weight * quad_ref[t, s]))
        for at in range(0, cols, tile):
            acc = ring[t + HALO, pl.ds(at + HALO, tile), :]
            for row, shift, coef in taps:
                acc = acc + coef * ring[row, pl.ds(at + shift, tile), :]
            out_ref[i, pl.ds(at, tile), :] = acc.astype(BF16)


def window(place, neighbour, basis, quad, low, high, disco, arrays, cols, waits):
    rows = sum(a.shape[0] for a in arrays)
    _, padded, cw = low.shape
    per_step = step_rows(rows, 2)
    return pl.pallas_call(
        functools.partial(window_kernel, cols, len(arrays)),
        grid=(rows // per_step,),
        in_specs=[smem_spec()] * 4
        + [whole_of(a) for a in (low, high, disco, *arrays)]
        + [any_spec()] * len(waits),
        out_specs=pl.BlockSpec((per_step, cols, cw), lambda t: (t, 0, 0)),
        out_shape=jax.ShapeDtypeStruct((rows, cols, cw), BF16),
        scratch_shapes=[pltpu.VMEM((rows + 2 * HALO, padded, cw), F32)],
        compiler_params=params(),
        cost_estimate=cost(0, 20000000),
    )(place, neighbour, basis, quad, low, high, disco, *arrays, *waits)


def mlp_kernel(place_ref, *refs):
    count = len(refs) - 9
    groups = refs[:count]
    gain_ref, w_in_ref, b_in_ref, w_out_ref, b_out_ref, field_ref, out_ref, spatial_ref, ordered = refs[count:]
    per_step, cols, cw = groups[0].shape
    for k in range(count):
        ordered[place_ref[k]] = groups[k][...].reshape(per_step * cols, cw)
    spatial = jnp.concatenate([ordered[k] for k in range(count)], axis=1)
    spatial_ref[...] = spatial.reshape(spatial_ref.shape)
    tokens = spatial.astype(F32)
    center = jnp.mean(tokens, axis=1, keepdims=True)
    shifted = tokens - center
    spread = jnp.mean(shifted * shifted, axis=1, keepdims=True)
    normed = (shifted * lax.rsqrt(spread + 1e-05) * gain_ref[...]).astype(BF16)
    hidden = jnp.dot(normed, w_in_ref[...], preferred_element_type=F32) + b_in_ref[...]
    hidden = jax.nn.gelu(hidden).astype(BF16)
    result = jnp.dot(hidden, w_out_ref[...], preferred_element_type=F32)
    result = result + b_out_ref[...] + field_ref[...].reshape(tokens.shape).astype(F32)
    out_ref[...] = result.astype(BF16).reshape(out_ref.shape)


def mlp(place, groups, gain, w_in, b_in, w_out, b_out, field):
    rows, cols, channels = field.shape
    cw = groups[0].shape[2]
    per_step = step_rows(rows, 2)
    block = pl.BlockSpec((per_step, cols, channels), lambda t: (t, 0, 0))
    part = pl.BlockSpec((per_step, cols, cw), lambda t: (t, 0, 0))
    return pl.pallas_call(
        mlp_kernel,
        grid=(rows // per_step,),
        in_specs=[smem_spec()]
        + [part] * len(groups)
        + [whole_of(a) for a in (gain, w_in, b_in, w_out, b_out)]
        + [block],
        out_specs=[block, block],
        out_shape=[jax.ShapeDtypeStruct(field.shape, BF16)] * 2,
        scratch_shapes=[pltpu.VMEM((len(groups), per_step * cols, cw), BF16)],
        compiler_params=params(),
        cost_estimate=cost(
            4 * field.size * w_in.shape[1], 8 * field.size, rows * cols * w_in.shape[1]
        ),
    )(place, *groups, gain, w_in, b_in, w_out, b_out, field)


def swap(array, axis, mask):
    count = lax.axis_size(axis)
    return lax.ppermute(array, axis, [(i, i ^ mask) for i in range(count)])


def shards(
    field,
    quad_weight,
    legendre,
    filter_real,
    filter_imag,
    neighbour,
    basis,
    disco_quad,
    disco_weight,
    norm_gain,
    w_in,
    b_in,
    w_out,
    b_out,
):
    rows, cols, channels = field.shape
    lon_count = lax.axis_size("lon")
    lat_count = lax.axis_size("lat")
    nz = lat_count // NQ
    wave_block, degrees, nlat = legendre.shape
    wave_rows = 2 * wave_block
    mmax = wave_block * lat_count
    nlon = cols * lon_count
    cblock = channels // lon_count
    nch = max(1, cblock // LANES)
    cw = cblock // nch
    padded_cols = (cols + 2 * HALO + 7) // 8 * 8
    lat_id = lax.axis_index("lat")
    lon_id = lax.axis_index("lon")

    fwd, inv = tables_np(nlon, lon_count, wave_block, mmax, padded_cols)
    zq = np.arange(lat_count)
    qz = (zq % nz) * NQ + zq // nz

    def permutation(masks, width):
        source = (lat_id ^ jnp.asarray(masks, jnp.int32))[:, None] * width
        source = (source + jnp.arange(width, dtype=jnp.int32)[None, :]).reshape(-1)
        return (jnp.arange(lat_count * width, dtype=jnp.int32)[None, :] == source[:, None]).astype(BF16)

    perm_fwd = permutation(zq, wave_rows)
    perm_inv = permutation(qz, wave_rows)
    perm_lat = permutation(qz, rows)

    def forward_table(table):
        parts = [
            jnp.dot(
                perm_fwd,
                lax.dynamic_index_in_dim(jnp.asarray(table), lon_id ^ s, 0, keepdims=False),
                preferred_element_type=F32,
            )
            for s in range(lon_count)
        ]
        return jnp.concatenate(parts, axis=1).astype(BF16)

    def inverse_table(table):
        parts = [
            jnp.einsum(
                "kr,ur->ku",
                lax.dynamic_index_in_dim(jnp.asarray(table), lon_id ^ s, 0, keepdims=False),
                perm_inv,
                preferred_element_type=F32,
            )
            for s in range(lon_count)
        ]
        return jnp.concatenate(parts, axis=0).astype(BF16)

    fwd = forward_table(fwd)
    inv = inverse_table(inv)
    leg = jnp.einsum("mlt,ut->mlu", legendre, perm_lat, preferred_element_type=F32).astype(BF16)
    legt = jnp.einsum("mlt,ut->mul", legendre, perm_lat, preferred_element_type=F32).astype(BF16)

    def chunk_of(array, s, j):
        start = (lon_id ^ s) * cblock + j * cw
        return lax.dynamic_slice_in_dim(array, start, cw, array.ndim - 1)

    def along(blocks):
        return [swap(block, "lat", NQ * (d + 1)) for d, block in enumerate(blocks)]

    def across(blocks):
        return [swap(block, "lat", q + 1) for q, block in enumerate(blocks)]

    disco = disco_weight.reshape(disco_weight.shape[0], lon_count * nch, cw)
    disco = jnp.transpose(disco, (1, 0, 2))
    up = [(i, i + 1) for i in range(lat_count - 1)]
    down = [(i + 1, i) for i in range(lat_count - 1)]

    def convolved(arrays, first, last, s, j, waits):
        low = lax.ppermute(last, "lat", up)
        high = lax.ppermute(first, "lat", down)
        place = channel_index(s, j)
        done = window(
            place[None], neighbour, basis, disco_quad, low, high, disco, arrays, cols, waits
        )
        return place, done

    def channel_index(s, j):
        return ((lon_id ^ s) * nch + j).astype(jnp.int32)

    received, waits = [], []
    for j in range(nch):
        received.append(
            [
                swap(pick(field, channel_index(s, j), cw, waits), "lon", s)
                for s in range(1, lon_count)
            ]
        )
        waits = [fwd]
    gains = [(chunk_of(filter_real, 0, j), chunk_of(filter_imag, 0, j)) for j in range(nch)]
    spectra = []
    waits = [leg, legt, inv] + [gain for pair in gains for gain in pair]
    for j in range(nch):
        arrays = dft(
            field, channel_index(0, j), received[j], quad_weight, fwd, nz, wave_rows, cw, waits
        )
        spectra.append([arrays[0]] + along(arrays[1:]))
        waits = [spectra[-1][1]]
        latest = arrays[0]
    near = []
    waits = [latest]
    for j in range(nch):
        full = legendre_step(
            spectra[j], across(regroup(spectra[j], waits)), leg, legt, *gains[j], []
        )
        near.append([full[0]] + across(full[1:]))
        waits = []
    regroups = [regroup(blocks, []) for blocks in near]
    groups, sent, waits = [], [], []
    for j in range(nch):
        split = j == nch - 1
        own, first, last, *apart = inverse(
            near[j], along(regroups[j]), inv, lon_count, split, waits
        )
        each = 2 if split else 1
        sent.append(
            [
                [swap(part, "lon", s) for part in apart[each * (s - 1) : each * s]]
                for s in range(1, lon_count)
            ]
        )
        groups.append(convolved([own], first, last, 0, j, []))
        waits = [groups[-1][1]]
    for j in range(nch):
        waits = [done for _, done in groups] if j == nch - 1 else []
        for s, arrays in enumerate(sent[j], 1):
            first, last = arrays[0][:HALO], arrays[0][-HALO:]
            groups.append(convolved(arrays, first, last, s, j, waits))
    block_out, spatial = mlp(
        jnp.stack([place for place, _ in groups]),
        [done for _, done in groups],
        norm_gain[None, :],
        w_in,
        b_in[None, :],
        w_out,
        b_out[None, :],
        field,
    )
    return (block_out, spatial)


def solution(mesh):
    grid = P("lat", "lon", None)
    rows = P("lat", None)
    placed = (grid, P("lat"), P("lat", None, None), P(), P(), rows, rows, rows) + (P(),) * 6
    return jax.shard_map(
        shards,
        mesh=mesh,
        in_specs=placed,
        out_specs=(grid, grid),
        check_vma=False,
    )
```
